256 devices in a mesh: dp: 32 (over y, z), tensor: 8 (over x, core).
Axes of the slice: x: 4, y: 4, z: 8, core: 2. Of those that a mesh axis runs over, the one named last changes fastest.
Arguments:
- saved_master: float32 [8, 128, 73728], P('tensor', 'dp'), may hold values from -0.078125 to 0.078125
- saved_first: float32 [8, 128, 73728], P('tensor', 'dp'), may hold values from -6 to 6
- saved_second: float32 [8, 128, 73728], P('tensor', 'dp'), may hold values from 0.25 to 4
- piece_columns: int32 [8, 128], P('tensor'), may hold values from 1 to 96, 6144 in all within a row
- load_order: int32 [8, 128], P('tensor'), may hold values from 0 to 127, each once within a row
- context: bfloat16 [8192, 6144], P('dp', 'tensor'), may hold values from -6 to 6
- out_grad: bfloat16 [8192, 6144], P('dp'), may hold values from -0.26367188 to 0.26367188
- next_context: bfloat16 [16384, 6144], P('dp', 'tensor'), may hold values from -6 to 6
Outputs:
- new_master: float32 [6144, 6144], P(('tensor', 'dp'))
- new_first: float32 [6144, 6144], P(('tensor', 'dp'))
- new_second: float32 [6144, 6144], P(('tensor', 'dp'))
- activations: bfloat16 [16384, 6144], P('dp', 'tensor')
The draws below stay inside these ranges and needn't reach their ends.
Inputs may be any that keep to these rules, and one draw needn't show every extreme that they name: `piece_columns`: for each tensor index the pieces lie one after another in old-rank order and cover all 6144 columns; some piece holds exactly 96 columns. `load_order`: for each tensor index every old rank sits at exactly one saved position.
All inputs are finite; a program needn't handle non-finite values.
Results may differ from the reference program's by a relative error of at most 0.0049.
Values may be sent and summed in bfloat16 or wider, within the bound.
A program may use at most 128 MiB of HBM per device.

```python
import math
import jax
import jax.numpy as jnp
import numpy as np
from jax import lax

ROWS = 6144
D_OUT = 6144
OLD_DP = 128
PC_MAX = 96
ROWS_T = 768
TOKENS = 8192
NEXT_TOKENS = 16384
N_TENSOR = 8


def with_spikes(drawn, rng, source, target, blocks, factor):
    def block_of(dim):
        return (jnp.arange(drawn.shape[dim]) // (drawn.shape[dim] // blocks)).reshape((-1,) + (1,) * (drawn.ndim - 1 - dim))

    one_side = jax.random.permutation(rng, blocks)[block_of(target)]
    second = (block_of(target) + blocks // 2) % blocks
    return jnp.where((block_of(source) == one_side) | (block_of(source) == second), factor * drawn, drawn)


def shard_levels(own_key, dims, cuts, low, top_value):
    factor_of, own = 1.0, jax.random.fold_in(own_key, 6)
    for dim, parts in cuts:
        heights = jnp.exp(jax.random.uniform(jax.random.fold_in(own, dim), (parts,), jnp.float32, low / len(cuts), top_value / len(cuts)))
        factor_of = factor_of * jnp.repeat(heights, dims[dim] // parts).reshape([-1 if axis == dim else 1 for axis in range(len(dims))])
    return factor_of


def split_up(amount, total, reach, slope):
    weights = [(1 << 20) // math.isqrt(rank ** slope) + 1 for rank in range(2, amount + 1)]
    spare, counts = total - reach - (amount - 1), [1] * (amount - 1)
    while spare > 0:
        candidates = [i for i in range(amount - 1) if counts[i] < reach]
        mass, left = sum([weights[i] for i in candidates]), spare
        for i in candidates:
            extra = min(reach - counts[i], max(1, left * weights[i] // mass), spare)
            counts[i] = counts[i] + extra
            spare = spare - extra
    return np.array([reach] + counts)


def uneven(key, count, total, most, lean):
    if count == 2:
        one = jax.random.randint(key, (), max(1, total - most), min(most, total - 1) + 1)
        return jnp.stack([one, total - one])
    sizes = jnp.asarray(split_up(count, total, most, lean), jnp.int32)
    twos = (count - 1) // 2
    donor, receiver = sizes[1:1 + 2 * twos:2], sizes[2:2 + 2 * twos:2]
    slack = jnp.minimum(donor - 1, most - receiver)
    moved = jax.random.randint(jax.random.fold_in(key, 1), (twos,), 0, 1 << 20) % (slack + 1)
    sizes = sizes.at[1:1 + 2 * twos:2].set(donor - moved).at[2:2 + 2 * twos:2].set(receiver + moved)
    return sizes[jax.random.permutation(jax.random.fold_in(key, 2), count)]


def scatter_about(own_key, shape, scale, most, shards=(), held_as=jnp.bfloat16):
    entries = scale * jax.random.normal(own_key, shape, jnp.float32)
    if shards:
        entries = entries * shard_levels(own_key, shape, shards, -0.22, 0.18)
    return jnp.clip(entries, -most, most).astype(held_as)


def heavy_noise(rng, dims, spread, limit, pieces, heavy, kind=jnp.bfloat16):
    result = spread * jax.random.normal(rng, dims, jnp.float32)
    if pieces:
        result = result * shard_levels(rng, dims, pieces, -0.22, 0.18)
    return jnp.clip(with_spikes(result, jax.random.fold_in(rng, 3), *heavy), -limit, limit).astype(kind)


def setup_inputs(seed: int = 0) -> dict:
    streams_of = jax.random.split(jax.random.key(seed), 9)
    saved_master = scatter_about(streams_of[0], (N_TENSOR, OLD_DP, ROWS_T * PC_MAX), ROWS ** -0.5, 0.078125, ((0, 8), (1, 32)), jnp.float32)
    saved_first = scatter_about(streams_of[1], (N_TENSOR, OLD_DP, ROWS_T * PC_MAX), 1.0, 6.0, ((0, 8), (1, 32)), jnp.float32)
    saved_second = jnp.clip(jnp.exp(math.log(4.0) - 2.7725887 * jax.random.uniform(streams_of[2], (N_TENSOR, OLD_DP, ROWS_T * PC_MAX), jnp.float32) ** shard_levels(streams_of[2], (N_TENSOR, OLD_DP, ROWS_T * PC_MAX), ((0, 8), (1, 32)), -0.2, 0.2)), 0.25, 4.0)
    piece_columns = jax.vmap(lambda own: uneven(own, OLD_DP, D_OUT, PC_MAX, 2))(jax.random.split(streams_of[3], N_TENSOR)).reshape((N_TENSOR, OLD_DP)).astype(jnp.int32)
    load_order = jax.vmap(lambda own: jax.random.permutation(own, OLD_DP))(jax.random.split(streams_of[4], N_TENSOR)).reshape((N_TENSOR, OLD_DP)).astype(jnp.int32)
    context = heavy_noise(streams_of[5], (TOKENS, ROWS), 1.0, 6.0, ((0, 32), (1, 8)), (0, 1, 32, 2.75))
    out_grad = scatter_about(streams_of[6], (TOKENS, D_OUT), (4.0 / TOKENS ** 0.5), 0.26367188, ((0, 32),))
    next_context = scatter_about(streams_of[7], (NEXT_TOKENS, ROWS), 1.0, 6.0, ((0, 32), (1, 8)))
    return {"saved_master": saved_master, "saved_first": saved_first, "saved_second": saved_second, "piece_columns": piece_columns, "load_order": load_order, "context": context, "out_grad": out_grad, "next_context": next_context}


first_bias = 1.0 - 0.9 ** 20
second_bias = 1.0 - 0.95 ** 20

def unpack(saved_state, lengths, order):
    old_ranks = lengths.shape[0]
    starts = (jnp.cumsum(lengths) - lengths).astype(jnp.int32)
    columns = jnp.arange(D_OUT, dtype=jnp.int32)
    owner_rank = lax.optimization_barrier(jnp.sum((starts[None, :] <= columns[:, None]).astype(jnp.int32), axis=1)) - 1
    places = jnp.arange(old_ranks, dtype=jnp.int32)
    position = lax.optimization_barrier(jnp.sum(jnp.where(order[None, :] == places[:, None], places[None, :], 0), axis=1)).astype(jnp.int32)
    within = (columns - starts[owner_rank]).astype(jnp.int32)
    blocks = saved_state.reshape(old_ranks, ROWS // N_TENSOR, PC_MAX)
    picked = blocks[position[owner_rank], :, within]
    return picked.T

def reference(saved_master, saved_first, saved_second, piece_columns, load_order, context, out_grad, next_context):
    states = []
    for saved_state in (saved_master, saved_first, saved_second):
        parts_list = [unpack(saved_state[index], piece_columns[index], load_order[index]) for index in range(N_TENSOR)]
        states.append(jnp.concatenate(parts_list, axis=0))
    master, first_moment, second_moment = states
    gradient = jnp.dot(context.T, out_grad, preferred_element_type=jnp.float32)
    new_first = 0.9 * first_moment + 0.1 * gradient
    new_second = 0.95 * second_moment + 0.05 * gradient * gradient
    new_master = master - 0.01 * (new_first / first_bias) / (jnp.sqrt(new_second / second_bias) + 1e-08)
    weight = new_master.astype(jnp.bfloat16)
    activations = jnp.dot(next_context, weight, preferred_element_type=jnp.float32).astype(jnp.bfloat16)
    return (new_master, new_first, new_second, activations)
```

```python
import jax
import jax.numpy as jnp
from jax import lax
from jax.experimental import pallas as pl
from jax.experimental.pallas import tpu as pltpu
from jax.sharding import PartitionSpec as P

first_bias = 1.0 - 0.9**20
second_bias = 1.0 - 0.95**20

MESH = pl.DeviceIdType.MESH
BF = jnp.bfloat16
F32 = jnp.float32
NY, NZ = 4, 8
NT = 8
BAND = 24
WIDE = 384
GROUPS = 6
SROWS = 80
QUARTER = 1536
HALF = 768


def where_am_i():
    dp = lax.axis_index("dp")
    t = lax.axis_index("tensor")
    return dp, t, dp // NZ, lax.rem(dp, NZ)


def remote(src, dst, send, recv, device):
    return pltpu.make_async_remote_copy(
        src_ref=src, dst_ref=dst, send_sem=send, recv_sem=recv, device_id=device, device_id_type=MESH
    )


def kernel_a(
    sm, sf, ss, ctx, og, rx, gq,
    st, flat, tx, cg, ct, oq, grad, zs, zr, tot, ysb,
    load_sem, loc_sem, st_s, st_r, cx_s, cx_r, og_s, og_r, fw_s, fw_r, rs_s, rs_r, ya_s, ya_r,
):
    dp, t, y, z = where_am_i()
    core = lax.rem(t, 2)
    mate = t + 1 - 2 * core

    loads = [pltpu.make_async_copy(src, st.at[a], load_sem.at[a]) for a, src in enumerate((sm, sf, ss))]
    for copy in loads:
        copy.start()
    own_ctx = pltpu.make_async_copy(ctx, cg.at[pl.ds(y * 256, 256)], loc_sem.at[0])
    own_og = pltpu.make_async_copy(
        og.at[:, pl.ds(y * QUARTER, QUARTER)], oq.at[pl.ds(y * 256, 256)], loc_sem.at[1]
    )
    own_ctx.start()
    own_og.start()

    barrier = pltpu.get_barrier_semaphore()

    @pl.loop(1, 32)
    def _(i):
        pl.semaphore_signal(barrier, inc=1, device_id=(lax.rem(dp + i, 32), t), device_id_type=MESH)

    pl.semaphore_signal(barrier, inc=1, device_id=(dp, mate), device_id_type=MESH)
    pl.semaphore_wait(barrier, 32)

    def ctx_copy(k):
        to = lax.rem(y + k, NY)
        return remote(ctx, cg.at[pl.ds(y * 256, 256)], cx_s.at[k], cx_r.at[k], (to * NZ + z, t))

    def og_copy(k):
        to = lax.rem(y + k, NY)
        return remote(
            og.at[pl.ds(core * 128, 128), pl.ds(to * QUARTER, QUARTER)],
            oq.at[pl.ds(y * 256 + core * 128, 128)],
            og_s.at[k], og_r.at[k], (to * NZ + z, t),
        )

    def fw_copy(k):
        rows = pl.ds(lax.rem(y + NY - k, NY) * 256 + core * 128, 128)
        return remote(oq.at[rows], oq.at[rows], fw_s.at[k], fw_r.at[k], (dp, mate))

    for k in (2, 1, 3):
        og_copy(k).start()
        ctx_copy(k).start()

    for copy in loads:
        copy.wait()

    def state_copy(i):
        to = lax.rem(y + i // NZ, NY) * NZ + lax.rem(z + lax.rem(i, NZ), NZ)
        return to, remote(tx.at[to], rx.at[dp], st_s.at[i], st_r.at[i], (to, t))

    def build(to):
        for a in range(3):
            for g in range(GROUPS):
                flat[a * BAND + 4 * g : a * BAND + 4 * g + 4, :] = st[a, to * GROUPS + g]
        tx[to] = flat[...].astype(BF)

    flat[3 * BAND :, :] = jnp.zeros((SROWS - 3 * BAND, WIDE), F32)

    @pl.loop(1, 32)
    def _(i):
        to, copy = state_copy(i)
        build(to)
        copy.start()

    build(dp)
    own_state = pltpu.make_async_copy(tx.at[dp], rx.at[dp], loc_sem.at[2])
    own_state.start()

    own_ctx.wait()
    own_og.wait()

    def turn(source):
        ct[:, pl.ds(source * 256, 256)] = cg[pl.ds(source * 256, 256), :].T

    turn(y)
    for k in (1, 3, 2):
        og_copy(k).wait_recv()
        fw_copy(k).start()
    for k in (1, 3, 2):
        ctx_copy(k).wait_recv()
        turn(lax.rem(y + NY - k, NY))
    for k in (1, 3, 2):
        fw_copy(k).wait_recv()

    def chunk(dest, h):
        return jnp.concatenate(
            [grad[pl.ds((yy * NZ + dest) * BAND, BAND), h * HALF : (h + 1) * HALF] for yy in range(NY)], axis=0
        )

    def steps(d, h):
        return 4 if d == h else 3

    def ring_copy(d, h, s):
        to = lax.rem(z + (1 if d == 0 else NZ - 1), NZ)
        return remote(zs.at[d, h, s], zr.at[d, h, s], rs_s.at[d, h, s], rs_r.at[d, h, s], (y * NZ + to, t))

    def ring_send(d, h, s):
        sign = 1 if d == 0 else NZ - 1
        dest = lax.rem(z + sign * (steps(d, h) - s), NZ)
        value = chunk(dest, h)
        if s > 0:
            ring_copy(d, h, s - 1).wait_recv()
            value = value + zr[d, h, s - 1].astype(F32)
        zs[d, h, s] = value.astype(BF)
        ring_copy(d, h, s).start()

    for h in range(2):
        @pl.loop(0, 3)
        def _(n):
            cols = pl.ds(h * HALF + n * 256, 256)
            grad[:, cols] = jnp.dot(ct[...], oq[:, cols], preferred_element_type=F32)

        ring_send(h, h, 0)
        ring_send(1 - h, h, 0)

    for s in range(1, 4):
        for h in range(2):
            for d in (h, 1 - h):
                if s < steps(d, h):
                    ring_send(d, h, s)

    def out_copy(k, h):
        to = lax.rem(y + k, NY)
        return remote(ysb.at[k, h], gq.at[y, h], ya_s.at[k, h], ya_r.at[k, h], (to * NZ + z, t))

    own_out = []
    for h in range(2):
        value = chunk(z, h)
        for d in (1 - h, h):
            last = steps(d, h) - 1
            ring_copy(d, h, last).wait_recv()
            value = value + zr[d, h, last].astype(F32)
        tot[...] = value
        for k in (2, 1, 3, 0):
            rows = pl.ds(lax.rem(y + k, NY) * BAND, BAND)
            ysb[k, h] = jnp.concatenate([tot[rows, 0:WIDE], tot[rows, WIDE:HALF]], axis=0).astype(BF)
            if k:
                out_copy(k, h).start()
            else:
                own_out.append(pltpu.make_async_copy(ysb.at[0, h], gq.at[y, h], loc_sem.at[3 + h]))
                own_out[-1].start()

    for k in (1, 2, 3):
        og_copy(k).wait_send()
        ctx_copy(k).wait_send()
        fw_copy(k).wait_send()
    for h in range(2):
        for d in range(2):
            for s in range(steps(d, h)):
                ring_copy(d, h, s).wait_send()
        for k in (1, 2, 3):
            out_copy(k, h).wait()
        own_out[h].wait()
    own_state.wait()

    @pl.loop(1, 32)
    def _(i):
        _, copy = state_copy(i)
        copy.wait()


def run_a(sm, sf, ss, ctx, og):
    any_spec = pl.BlockSpec(memory_space=pl.ANY)
    dma = pltpu.SemaphoreType.DMA
    return pl.pallas_call(
        kernel_a,
        name="state_and_gradient",
        out_shape=(
            jax.ShapeDtypeStruct((32, SROWS, WIDE), BF),
            jax.ShapeDtypeStruct((NY, 2, 2 * BAND, WIDE), BF),
        ),
        in_specs=[any_spec] * 5,
        out_specs=(any_spec, any_spec),
        scratch_shapes=[
            pltpu.VMEM((3, 192, 4, WIDE), F32),
            pltpu.VMEM((SROWS, WIDE), F32),
            pltpu.VMEM((32, SROWS, WIDE), BF),
            pltpu.VMEM((1024, HALF), BF),
            pltpu.VMEM((HALF, 1024), BF),
            pltpu.VMEM((1024, QUARTER), BF),
            pltpu.VMEM((HALF, QUARTER), F32),
            pltpu.VMEM((2, 2, 4, 4 * BAND, HALF), BF),
            pltpu.VMEM((2, 2, 4, 4 * BAND, HALF), BF),
            pltpu.VMEM((4 * BAND, HALF), F32),
            pltpu.VMEM((4, 2, 2 * BAND, WIDE), BF),
            dma((3,)), dma((5,)),
            dma((32,)), dma((32,)),
            dma((4,)), dma((4,)), dma((4,)), dma((4,)), dma((4,)), dma((4,)),
            dma((2, 2, 4)), dma((2, 2, 4)),
            dma((4, 2)), dma((4, 2)),
        ],
        compiler_params=pltpu.CompilerParams(
            collective_id=0, has_side_effects=True, vmem_limit_bytes=48 * 2**20
        ),
        cost_estimate=pl.CostEstimate(flops=2 * 1024 * 768 * 1536, bytes_accessed=16 * 2**20, transcendentals=0),
    )(sm, sf, ss, ctx, og)


def kernel_b(pc, lo, rx, gq, nm, nf, ns, wb, zbuf, obuf, gbuf, mbuf, fbuf, sbuf, starts, sem):
    row = lax.broadcasted_iota(jnp.int32, (WIDE, 512), 0)
    col = lax.broadcasted_iota(jnp.int32, (WIDE, 512), 1)
    spread = ((row == (col // 128) * 96 + lax.rem(col, 128)) & (lax.rem(col, 128) < 96)).astype(BF)

    def count(j, total):
        starts[j] = total
        return total + pc[j]

    lax.fori_loop(0, 128, count, jnp.int32(0))

    @pl.loop(0, 10)
    def _(i):
        rows = pl.ds(i * 256, 256)
        value = jnp.dot(rx[rows, :], spread, preferred_element_type=F32)
        for r in range(4):
            zbuf[r, rows, :] = value[:, r * 128 : (r + 1) * 128]

    for yy in range(NY):
        for h in range(2):
            block = gq[yy, h].astype(F32)
            for q in range(2):
                c0 = yy * QUARTER + h * HALF + q * WIDE
                for n in range(3):
                    gbuf[c0 // 128 + n, 0:BAND, :] = block[q * BAND : (q + 1) * BAND, n * 128 : (n + 1) * 128]

    lane = lax.broadcasted_iota(jnp.int32, (8, 128), 1)

    @pl.loop(0, 128)
    def _(i):
        rank = lo[i]
        start = starts[rank]
        length = pc[rank]
        tile = start // 128
        offset = lax.rem(start, 128)
        keep = (lane >= offset) & (lane < offset + length)
        spill = lane < offset + length - 128
        base = (i // 4) * SROWS + lax.rem(i, 4)
        for a in range(3):
            for r in range(4):
                value = zbuf[r, pl.ds(base + a * BAND, 8, stride=4), :]
                value = pltpu.roll(value, offset, 1)
                pltpu.store(obuf.at[a * 4 + r, tile], value, mask=keep)
                pltpu.store(obuf.at[a * 4 + r, tile + 1], value, mask=spill)

    @pl.loop(0, 48)
    def _(n):
        cols = pl.ds(pl.multiple_of(n * 128, 128), 128)
        for r in range(4):
            rows = pl.ds(r, 8, stride=4)
            gradient = gbuf[n, rows, :]
            first = 0.9 * obuf[4 + r, n] + 0.1 * gradient
            second = 0.95 * obuf[8 + r, n] + 0.05 * gradient * gradient
            master = obuf[r, n] - 0.01 * (first / first_bias) / (jnp.sqrt(second / second_bias) + 1e-08)
            mbuf[n, rows, :] = master
            fbuf[n, rows, :] = first
            sbuf[n, rows, :] = second
        nm[:, cols] = mbuf[n, 0:BAND, :]
        nf[:, cols] = fbuf[n, 0:BAND, :]
        ns[:, cols] = sbuf[n, 0:BAND, :]

    for t in range(NT):
        wb[t] = jnp.concatenate(
            [nm[:, t * HALF : t * HALF + WIDE], nm[:, t * HALF + WIDE : (t + 1) * HALF]], axis=0
        ).astype(BF)


def run_b(pc, lo, rx, gq):
    smem = pl.BlockSpec(memory_space=pltpu.SMEM)
    vmem = pl.BlockSpec(memory_space=pltpu.VMEM)
    state = jax.ShapeDtypeStruct((BAND, 6144), F32)
    return pl.pallas_call(
        kernel_b,
        name="place_and_adam",
        out_shape=(state, state, state, jax.ShapeDtypeStruct((NT, 2 * BAND, WIDE), BF)),
        in_specs=[smem, smem, vmem, vmem],
        out_specs=(vmem, vmem, vmem, vmem),
        scratch_shapes=[
            pltpu.VMEM((4, 32 * SROWS + 32, 128), F32),
            pltpu.VMEM((12, 50, 8, 128), F32),
            pltpu.VMEM((48, 32, 128), F32),
            pltpu.VMEM((48, 32, 128), F32),
            pltpu.VMEM((48, 32, 128), F32),
            pltpu.VMEM((48, 32, 128), F32),
            pltpu.SMEM((128,), jnp.int32),
            pltpu.SemaphoreType.DMA((1,)),
        ],
        compiler_params=pltpu.CompilerParams(vmem_limit_bytes=40 * 2**20),
        cost_estimate=pl.CostEstimate(flops=10**9, bytes_accessed=5 * 2**20, transcendentals=0),
    )(pc, lo, rx, gq)


ZT = 5


def kernel_c(
    wb, nc, out, wg, wn, nv,
    nc_sem, own_sem, w1_s, w1_r, y1_s, y1_r, zz_s, zz_r, zy_s, zy_r, yz_s, yz_r,
):
    dp, t, y, z = where_am_i()
    load = pltpu.make_async_copy(nc, nv, nc_sem.at[0])
    load.start()
    own = pltpu.make_async_copy(wb.at[t], wg.at[y, z, t], own_sem.at[0])
    own.start()

    barrier = pltpu.get_barrier_semaphore()
    for k in range(1, NT):
        pl.semaphore_signal(barrier, inc=1, device_id=(dp, lax.rem(t + k, NT)), device_id_type=MESH)
    for k in range(1, NY):
        pl.semaphore_signal(
            barrier, inc=1, device_id=(lax.rem(y + k, NY) * NZ + z, t), device_id_type=MESH
        )
    for k in (1, NZ - 1):
        pl.semaphore_signal(
            barrier, inc=1, device_id=(y * NZ + lax.rem(z + k, NZ), t), device_id_type=MESH
        )
    pl.semaphore_wait(barrier, NT - 1 + NY - 1 + 2)

    def first_copy(k):
        to = lax.rem(t + k, NT)
        return remote(wb.at[to], wg.at[y, z, t], w1_s.at[k], w1_r.at[k], (dp, to))

    for k in range(1, NT):
        first_copy(k).start()
    own.wait()
    for k in range(1, NT):
        first_copy(k).wait()

    def over_y(k):
        piece = wg.at[y, z, pl.ds(ZT, NT - ZT)]
        return remote(piece, piece, y1_s.at[k], y1_r.at[k], (lax.rem(y + k, NY) * NZ + z, t))

    def around(d, s, part):
        sign = 1 if d == 0 else NZ - 1
        owner = lax.rem(z + (NZ - sign) * s, NZ)
        to = y * NZ + lax.rem(z + sign, NZ)
        if part == 0:
            piece = wg.at[y, owner, pl.ds(0, ZT)]
            return remote(piece, piece, zz_s.at[d, s], zz_r.at[d, s], (to, t))
        piece = wg.at[:, owner, pl.ds(ZT, NT - ZT)]
        return remote(piece, piece, yz_s.at[d, s], yz_r.at[d, s], (to, t))

    def steps(d, part):
        return 4 if d == part else 3

    def across(d, owner):
        sign = 1 if d == 0 else NY - 1
        piece = wg.at[y, owner, pl.ds(0, ZT)]
        return remote(
            piece, piece, zy_s.at[d, owner], zy_r.at[d, owner], (lax.rem(y + sign, NY) * NZ + z, t)
        )

    def onward(owner):
        odd = lax.rem(owner, 2)
        source = lax.rem(y + NY - 1 + 2 * odd, NY)
        target = lax.rem(y + 1 + 2 * odd, NY)
        piece = wg.at[source, owner, pl.ds(0, ZT)]
        return remote(piece, piece, zy_s.at[2, owner], zy_r.at[2, owner], (target * NZ + z, t))

    def spread(owner):
        across(0, owner).start()
        across(1, owner).start()

    def pass_on(owner):
        across(0, owner).wait_recv()
        across(1, owner).wait_recv()
        onward(owner).start()

    for k in (2, 1, 3):
        over_y(k).start()
    around(0, 0, 0).start()
    around(1, 0, 0).start()
    spread(z)
    for k in (1, 3, 2):
        over_y(k).wait_recv()
    around(0, 0, 1).start()
    around(1, 0, 1).start()

    done = [z]
    for s in range(1, 5):
        fresh = []
        for part in range(2):
            for d in range(2):
                if s - 1 < steps(d, part):
                    around(d, s - 1, part).wait_recv()
                    if s < steps(d, part):
                        around(d, s, part).start()
                    if part == 0:
                        sign = 1 if d == 0 else NZ - 1
                        owner = lax.rem(z + (NZ - sign) * s, NZ)
                        spread(owner)
                        fresh.append(owner)
        for owner in done:
            pass_on(owner)
        done = fresh
    for owner in done:
        pass_on(owner)

    @pl.loop(0, NZ)
    def _(owner):
        onward(owner).wait()
        across(0, owner).wait_send()
        across(1, owner).wait_send()

    for k in range(1, NY):
        over_y(k).wait_send()
    for d in range(2):
        for part in range(2):
            for s in range(steps(d, part)):
                around(d, s, part).wait_send()

    @pl.loop(0, NT)
    def _(tt):
        @pl.loop(0, 16)
        def _(pair):
            yy = pair // 4
            zz = lax.rem(pair, 4) * 2
            a = wg[yy, zz, tt].astype(F32)
            b = wg[yy, zz + 1, tt].astype(F32)
            rows = pl.ds(pl.multiple_of(pair * 48, 48), 48)
            wn[tt, rows, 0:WIDE] = jnp.concatenate([a[:BAND], b[:BAND]], axis=0).astype(BF)
            wn[tt, rows, WIDE:HALF] = jnp.concatenate([a[BAND:], b[BAND:]], axis=0).astype(BF)

    load.wait()

    @pl.loop(0, 3)
    def _(n):
        cols = pl.ds(pl.multiple_of(n * 256, 256), 256)
        total = jnp.dot(nv[0], wn[0, :, cols], preferred_element_type=F32)
        for tt in range(1, NT):
            total = total + jnp.dot(nv[tt], wn[tt, :, cols], preferred_element_type=F32)
        out[:, cols] = total.astype(BF)


def run_c(wb, nc):
    any_spec = pl.BlockSpec(memory_space=pl.ANY)
    vmem = pl.BlockSpec(memory_space=pltpu.VMEM)
    dma = pltpu.SemaphoreType.DMA
    return pl.pallas_call(
        kernel_c,
        name="weights_and_product",
        out_shape=jax.ShapeDtypeStruct((512, HALF), BF),
        in_specs=[vmem, any_spec],
        out_specs=vmem,
        scratch_shapes=[
            pltpu.VMEM((NY, NZ, NT, 2 * BAND, WIDE), BF),
            pltpu.VMEM((NT, HALF, HALF), BF),
            pltpu.VMEM((NT, 512, HALF), BF),
            dma((1,)), dma((1,)),
            dma((8,)), dma((8,)),
            dma((4,)), dma((4,)),
            dma((2, 4)), dma((2, 4)),
            dma((3, 8)), dma((3, 8)),
            dma((2, 4)), dma((2, 4)),
        ],
        compiler_params=pltpu.CompilerParams(
            collective_id=1, has_side_effects=True, vmem_limit_bytes=48 * 2**20
        ),
        cost_estimate=pl.CostEstimate(flops=2 * 512 * 6144 * 768, bytes_accessed=8 * 2**20, transcendentals=0),
    )(wb, nc)


def shards(
    saved_master,
    saved_first,
    saved_second,
    piece_columns,
    load_order,
    context,
    out_grad,
    next_context,
):
    def grouped(saved):
        return saved[0].reshape(4, 192, WIDE).transpose(1, 0, 2)

    tokens = lax.all_gather(next_context, "tensor")
    rx, gq = run_a(grouped(saved_master), grouped(saved_first), grouped(saved_second), context, out_grad)
    new_master, new_first, new_second, blocks = run_b(
        piece_columns[0], load_order[0], rx.reshape(32 * SROWS, WIDE), gq
    )
    activations = run_c(blocks, tokens)
    return (new_master, new_first, new_second, activations)


def solution(mesh):
    placed = (
        P("tensor", "dp", None),
        P("tensor", "dp", None),
        P("tensor", "dp", None),
        P("tensor", None),
        P("tensor", None),
        P("dp", "tensor"),
        P("dp", None),
        P("dp", "tensor"),
    )
    return jax.shard_map(
        shards,
        mesh=mesh,
        in_specs=placed,
        out_specs=(
            P(("tensor", "dp"), None),
            P(("tensor", "dp"), None),
            P(("tensor", "dp"), None),
            P("dp", "tensor"),
        ),
        check_vma=False,
    )
```

```python
import jax
import jax.numpy as jnp
from jax import lax
from jax.experimental import pallas as pl
from jax.experimental.pallas import tpu as pltpu
from jax.sharding import PartitionSpec as P

first_bias = 1.0 - 0.9**20
second_bias = 1.0 - 0.95**20

MESH = pl.DeviceIdType.MESH
BF = jnp.bfloat16
F32 = jnp.float32
NY, NZ = 4, 8
NT = 8
BAND = 24
WIDE = 384
GROUPS = 6
SROWS = 72
QUARTER = 1536
HALF = 768


def where_am_i():
    dp = lax.axis_index("dp")
    t = lax.axis_index("tensor")
    return dp, t, dp // NZ, lax.rem(dp, NZ)


def remote(src, dst, send, recv, device):
    return pltpu.make_async_remote_copy(
        src_ref=src, dst_ref=dst, send_sem=send, recv_sem=recv, device_id=device, device_id_type=MESH
    )


VMEM_A = 60 * 2**20


def kernel_a(
    sm, sf, ss, ctx, og, rx, gq,
    st, flat, tx, mid, ty, cg, ct, oq, grad, zs, zr, tot, ysb,
    load_sem, loc_sem, st_s, st_r, sy_s, sy_r, cx_s, cx_r, og_s, og_r, fw_s, fw_r, rs_s, rs_r, ya_s, ya_r,
):
    dp, t, y, z = where_am_i()
    core = lax.rem(t, 2)
    mate = t + 1 - 2 * core

    loads = [pltpu.make_async_copy(src, st.at[a], load_sem.at[a]) for a, src in enumerate((sm, sf, ss))]
    for copy in loads:
        copy.start()
    own_ctx = pltpu.make_async_copy(ctx, cg.at[pl.ds(y * 256, 256)], loc_sem.at[0])
    own_og = pltpu.make_async_copy(
        og.at[:, pl.ds(y * QUARTER, QUARTER)], oq.at[pl.ds(y * 256, 256)], loc_sem.at[1]
    )
    own_ctx.start()
    own_og.start()

    barrier = pltpu.get_barrier_semaphore()

    for k in range(1, NY):
        pl.semaphore_signal(
            barrier, inc=1, device_id=(lax.rem(y + k, NY) * NZ + z, t), device_id_type=MESH
        )
    for k in range(1, NZ):
        pl.semaphore_signal(
            barrier, inc=1, device_id=(y * NZ + lax.rem(z + k, NZ), t), device_id_type=MESH
        )
    pl.semaphore_signal(barrier, inc=1, device_id=(dp, mate), device_id_type=MESH)
    pl.semaphore_wait(barrier, NY - 1 + NZ - 1 + 1)

    def ctx_copy(k):
        to = lax.rem(y + k, NY)
        return remote(ctx, cg.at[pl.ds(y * 256, 256)], cx_s.at[k], cx_r.at[k], (to * NZ + z, t))

    def og_copy(k):
        to = lax.rem(y + k, NY)
        return remote(
            og.at[pl.ds(core * 128, 128), pl.ds(to * QUARTER, QUARTER)],
            oq.at[pl.ds(y * 256 + core * 128, 128)],
            og_s.at[k], og_r.at[k], (to * NZ + z, t),
        )

    def fw_copy(k):
        rows = pl.ds(lax.rem(y + NY - k, NY) * 256 + core * 128, 128)
        return remote(oq.at[rows], oq.at[rows], fw_s.at[k], fw_r.at[k], (dp, mate))

    for k in (2, 1, 3):
        og_copy(k).start()
        ctx_copy(k).start()

    for copy in loads:
        copy.wait()

    def state_copy(k):
        to = lax.rem(z + k, NZ)
        return remote(tx.at[k], mid.at[z], st_s.at[k], st_r.at[k], (y * NZ + to, t))

    def build(k):
        for ky in range(NY):
            owner = lax.rem(y + ky, NY) * NZ + lax.rem(z + k, NZ)
            for a in range(3):
                for g in range(GROUPS):
                    row = ky * SROWS + a * BAND + 4 * g
                    flat[row : row + 4, :] = st[a, owner * GROUPS + g]
        return flat[...].astype(BF)

    for k in (4, 3, 5, 2, 6, 1, 7):
        tx[k] = build(k)
        state_copy(k).start()
    mid[z] = build(0)

    def state_over_y(k, pair):
        to = lax.rem(y + k, NY) * NZ + z
        return remote(ty.at[pair, k], rx.at[y * 4 + pair], sy_s.at[pair, k], sy_r.at[pair, k], (to, t))

    def state_local(pair):
        return pltpu.make_async_copy(ty.at[pair, 0], rx.at[y * 4 + pair], loc_sem.at[5 + pair])

    def pass_state(pair):
        low = mid[2 * pair].astype(F32)
        high = mid[2 * pair + 1].astype(F32)
        for k in (2, 1, 3, 0):
            rows = slice(k * SROWS, (k + 1) * SROWS)
            ty[pair, k] = jnp.concatenate([low[rows], high[rows]], axis=0).astype(BF)
            if k:
                state_over_y(k, pair).start()
            else:
                state_local(pair).start()

    own_ctx.wait()
    own_og.wait()

    def turn(source):
        ct[:, pl.ds(source * 256, 256)] = cg[pl.ds(source * 256, 256), :].T

    turn(y)
    for k in (1, 3, 2):
        og_copy(k).wait_recv()
        fw_copy(k).start()
    for k in (1, 3, 2):
        ctx_copy(k).wait_recv()
        turn(lax.rem(y + NY - k, NY))
    for k in (1, 3, 2):
        fw_copy(k).wait_recv()

    def chunk(dest, h):
        return jnp.concatenate(
            [grad[pl.ds((yy * NZ + dest) * BAND, BAND), h * HALF : (h + 1) * HALF] for yy in range(NY)], axis=0
        )

    def steps(d, h):
        return 4 if d == h else 3

    def ring_copy(d, h, s):
        to = lax.rem(z + (1 if d == 0 else NZ - 1), NZ)
        return remote(zs.at[d, h, s], zr.at[d, h, s], rs_s.at[d, h, s], rs_r.at[d, h, s], (y * NZ + to, t))

    def ring_send(d, h, s):
        sign = 1 if d == 0 else NZ - 1
        dest = lax.rem(z + sign * (steps(d, h) - s), NZ)
        value = chunk(dest, h)
        if s > 0:
            ring_copy(d, h, s - 1).wait_recv()
            value = value + zr[d, h, s - 1].astype(F32)
        zs[d, h, s] = value.astype(BF)
        ring_copy(d, h, s).start()

    for h in range(2):
        @pl.loop(0, 3)
        def _(n):
            cols = pl.ds(h * HALF + n * 256, 256)
            grad[:, cols] = jnp.dot(ct[...], oq[:, cols], preferred_element_type=F32)

        ring_send(h, h, 0)
        ring_send(1 - h, h, 0)

    for s in range(1, 4):
        for h in range(2):
            for d in (h, 1 - h):
                if s < steps(d, h):
                    ring_send(d, h, s)
        if s == 1:
            for k in (1, 7, 2, 6, 3, 5, 4):
                state_copy(k).wait_recv()
        for pair in ((0, 1), (2, 3), ())[s - 1]:
            pass_state(pair)

    def out_copy(k, h):
        to = lax.rem(y + k, NY)
        return remote(ysb.at[k, h], gq.at[y, h], ya_s.at[k, h], ya_r.at[k, h], (to * NZ + z, t))

    own_out = []
    for h in range(2):
        value = chunk(z, h)
        for d in (1 - h, h):
            last = steps(d, h) - 1
            ring_copy(d, h, last).wait_recv()
            value = value + zr[d, h, last].astype(F32)
        tot[...] = value
        for k in (2, 1, 3, 0):
            rows = pl.ds(lax.rem(y + k, NY) * BAND, BAND)
            ysb[k, h] = jnp.concatenate([tot[rows, 0:WIDE], tot[rows, WIDE:HALF]], axis=0).astype(BF)
            if k:
                out_copy(k, h).start()
            else:
                own_out.append(pltpu.make_async_copy(ysb.at[0, h], gq.at[y, h], loc_sem.at[3 + h]))
                own_out[-1].start()

    for k in (1, 2, 3):
        og_copy(k).wait_send()
        ctx_copy(k).wait_send()
        fw_copy(k).wait_send()
    for h in range(2):
        for d in range(2):
            for s in range(steps(d, h)):
                ring_copy(d, h, s).wait_send()
        for k in (1, 2, 3):
            out_copy(k, h).wait()
        own_out[h].wait()
    for k in range(1, NZ):
        state_copy(k).wait_send()
    for pair in range(4):
        for k in (1, 2, 3):
            state_over_y(k, pair).wait()
        state_local(pair).wait()


def run_a(sm, sf, ss, ctx, og):
    any_spec = pl.BlockSpec(memory_space=pl.ANY)
    dma = pltpu.SemaphoreType.DMA
    return pl.pallas_call(
        kernel_a,
        name="state_and_gradient",
        out_shape=(
            jax.ShapeDtypeStruct((16, 2 * SROWS, WIDE), BF),
            jax.ShapeDtypeStruct((NY, 2, 2 * BAND, WIDE), BF),
        ),
        in_specs=[any_spec] * 5,
        out_specs=(any_spec, any_spec),
        scratch_shapes=[
            pltpu.VMEM((3, 192, 4, WIDE), F32),
            pltpu.VMEM((4 * SROWS, WIDE), F32),
            pltpu.VMEM((NZ, 4 * SROWS, WIDE), BF),
            pltpu.VMEM((NZ, 4 * SROWS, WIDE), BF),
            pltpu.VMEM((4, NY, 2 * SROWS, WIDE), BF),
            pltpu.VMEM((1024, HALF), BF),
            pltpu.VMEM((HALF, 1024), BF),
            pltpu.VMEM((1024, QUARTER), BF),
            pltpu.VMEM((HALF, QUARTER), F32),
            pltpu.VMEM((2, 2, 4, 4 * BAND, HALF), BF),
            pltpu.VMEM((2, 2, 4, 4 * BAND, HALF), BF),
            pltpu.VMEM((4 * BAND, HALF), F32),
            pltpu.VMEM((4, 2, 2 * BAND, WIDE), BF),
            dma((3,)), dma((9,)),
            dma((8,)), dma((8,)),
            dma((4, 4)), dma((4, 4)),
            dma((4,)), dma((4,)), dma((4,)), dma((4,)), dma((4,)), dma((4,)),
            dma((2, 2, 4)), dma((2, 2, 4)),
            dma((4, 2)), dma((4, 2)),
        ],
        compiler_params=pltpu.CompilerParams(
            collective_id=0, has_side_effects=True, vmem_limit_bytes=VMEM_A
        ),
        cost_estimate=pl.CostEstimate(flops=2 * 1024 * 768 * 1536, bytes_accessed=16 * 2**20, transcendentals=0),
    )(sm, sf, ss, ctx, og)


def kernel_b(pc, lo, rx, gq, nm, nf, ns, wb, zbuf, obuf, gbuf, mbuf, fbuf, sbuf, starts):
    row = lax.broadcasted_iota(jnp.int32, (WIDE, 512), 0)
    col = lax.broadcasted_iota(jnp.int32, (WIDE, 512), 1)
    spread = ((row == (col // 128) * 96 + lax.rem(col, 128)) & (lax.rem(col, 128) < 96)).astype(BF)

    def count(j, total):
        starts[j] = total
        return total + pc[j]

    lax.fori_loop(0, 128, count, jnp.int32(0))

    @pl.loop(0, 9)
    def _(i):
        rows = pl.ds(i * 256, 256)
        value = jnp.dot(rx[rows, :], spread, preferred_element_type=F32)
        for r in range(4):
            zbuf[r, rows, :] = value[:, r * 128 : (r + 1) * 128]

    for yy in range(NY):
        for h in range(2):
            block = gq[yy, h].astype(F32)
            for q in range(2):
                c0 = yy * QUARTER + h * HALF + q * WIDE
                for n in range(3):
                    gbuf[c0 // 128 + n, 0:BAND, :] = block[q * BAND : (q + 1) * BAND, n * 128 : (n + 1) * 128]

    lane = lax.broadcasted_iota(jnp.int32, (8, 128), 1)

    @pl.loop(0, 128, unroll=4)
    def _(i):
        rank = lo[i]
        start = starts[rank]
        length = pc[rank]
        tile = start // 128
        offset = lax.rem(start, 128)
        keep = (lane >= offset) & (lane < offset + length)
        spill = lane < offset + length - 128
        base = (i // 4) * SROWS + lax.rem(i, 4)
        for a in range(3):
            for r in range(4):
                value = zbuf[r, pl.ds(base + a * BAND, 8, stride=4), :]
                value = pltpu.roll(value, offset, 1)
                pltpu.store(obuf.at[a * 4 + r, tile], value, mask=keep)
                pltpu.store(obuf.at[a * 4 + r, tile + 1], value, mask=spill)

    @pl.loop(0, 48, unroll=4)
    def _(n):
        cols = pl.ds(pl.multiple_of(n * 128, 128), 128)
        for r in range(4):
            rows = pl.ds(r, 8, stride=4)
            gradient = gbuf[n, rows, :]
            first = 0.9 * obuf[4 + r, n] + 0.1 * gradient
            second = 0.95 * obuf[8 + r, n] + 0.05 * gradient * gradient
            master = obuf[r, n] - 0.01 * (first / first_bias) / (jnp.sqrt(second / second_bias) + 1e-08)
            mbuf[n, rows, :] = master
            fbuf[n, rows, :] = first
            sbuf[n, rows, :] = second
        nm[:, cols] = mbuf[n, 0:BAND, :]
        nf[:, cols] = fbuf[n, 0:BAND, :]
        ns[:, cols] = sbuf[n, 0:BAND, :]

    for t in range(NT):
        wb[t] = jnp.concatenate(
            [nm[:, t * HALF : t * HALF + WIDE], nm[:, t * HALF + WIDE : (t + 1) * HALF]], axis=0
        ).astype(BF)


def run_b(pc, lo, rx, gq):
    smem = pl.BlockSpec(memory_space=pltpu.SMEM)
    vmem = pl.BlockSpec(memory_space=pltpu.VMEM)
    state = jax.ShapeDtypeStruct((BAND, 6144), F32)
    return pl.pallas_call(
        kernel_b,
        name="place_and_adam",
        out_shape=(state, state, state, jax.ShapeDtypeStruct((NT, 2 * BAND, WIDE), BF)),
        in_specs=[smem, smem, vmem, vmem],
        out_specs=(vmem, vmem, vmem, vmem),
        scratch_shapes=[
            pltpu.VMEM((4, 32 * SROWS + 32, 128), F32),
            pltpu.VMEM((12, 50, 8, 128), F32),
            pltpu.VMEM((48, 32, 128), F32),
            pltpu.VMEM((48, 32, 128), F32),
            pltpu.VMEM((48, 32, 128), F32),
            pltpu.VMEM((48, 32, 128), F32),
            pltpu.SMEM((128,), jnp.int32),
        ],
        compiler_params=pltpu.CompilerParams(vmem_limit_bytes=40 * 2**20),
        cost_estimate=pl.CostEstimate(flops=10**9, bytes_accessed=5 * 2**20, transcendentals=0),
    )(pc, lo, rx, gq)


ZT = 5


def kernel_c(
    wb, nc, out, wg, wn, nv,
    nc_sem, own_sem, w1_s, w1_r, y1_s, y1_r, zz_s, zz_r, zy_s, zy_r, yz_s, yz_r,
):
    dp, t, y, z = where_am_i()
    load = pltpu.make_async_copy(nc, nv, nc_sem.at[0])
    load.start()
    own = pltpu.make_async_copy(wb.at[t], wg.at[y, z, t], own_sem.at[0])
    own.start()

    barrier = pltpu.get_barrier_semaphore()
    for k in range(1, NT):
        pl.semaphore_signal(barrier, inc=1, device_id=(dp, lax.rem(t + k, NT)), device_id_type=MESH)
    for k in range(1, NY):
        pl.semaphore_signal(
            barrier, inc=1, device_id=(lax.rem(y + k, NY) * NZ + z, t), device_id_type=MESH
        )
    for k in (1, NZ - 1):
        pl.semaphore_signal(
            barrier, inc=1, device_id=(y * NZ + lax.rem(z + k, NZ), t), device_id_type=MESH
        )
    pl.semaphore_wait(barrier, NT - 1 + NY - 1 + 2)

    def first_copy(k):
        to = lax.rem(t + k, NT)
        return remote(wb.at[to], wg.at[y, z, t], w1_s.at[k], w1_r.at[k], (dp, to))

    for k in range(1, NT):
        first_copy(k).start()
    own.wait()
    for k in range(1, NT):
        first_copy(k).wait()

    def over_y(k):
        piece = wg.at[y, z, pl.ds(ZT, NT - ZT)]
        return remote(piece, piece, y1_s.at[k], y1_r.at[k], (lax.rem(y + k, NY) * NZ + z, t))

    def around(d, s, part):
        sign = 1 if d == 0 else NZ - 1
        owner = lax.rem(z + (NZ - sign) * s, NZ)
        to = y * NZ + lax.rem(z + sign, NZ)
        if part == 0:
            piece = wg.at[y, owner, pl.ds(0, ZT)]
            return remote(piece, piece, zz_s.at[d, s], zz_r.at[d, s], (to, t))
        piece = wg.at[:, owner, pl.ds(ZT, NT - ZT)]
        return remote(piece, piece, yz_s.at[d, s], yz_r.at[d, s], (to, t))

    def steps(d, part):
        return 4 if d == part else 3

    def across(d, owner):
        sign = 1 if d == 0 else NY - 1
        piece = wg.at[y, owner, pl.ds(0, ZT)]
        return remote(
            piece, piece, zy_s.at[d, owner], zy_r.at[d, owner], (lax.rem(y + sign, NY) * NZ + z, t)
        )

    def onward(owner):
        odd = lax.rem(owner, 2)
        source = lax.rem(y + NY - 1 + 2 * odd, NY)
        target = lax.rem(y + 1 + 2 * odd, NY)
        piece = wg.at[source, owner, pl.ds(0, ZT)]
        return remote(piece, piece, zy_s.at[2, owner], zy_r.at[2, owner], (target * NZ + z, t))

    def spread(owner):
        across(0, owner).start()
        across(1, owner).start()

    def pass_on(owner):
        across(0, owner).wait_recv()
        across(1, owner).wait_recv()
        onward(owner).start()

    for k in (2, 1, 3):
        over_y(k).start()
    around(0, 0, 0).start()
    around(1, 0, 0).start()
    spread(z)
    for k in (1, 3, 2):
        over_y(k).wait_recv()
    around(0, 0, 1).start()
    around(1, 0, 1).start()

    done = [z]
    for s in range(1, 5):
        fresh = []
        for part in range(2):
            for d in range(2):
                if s - 1 < steps(d, part):
                    around(d, s - 1, part).wait_recv()
                    if s < steps(d, part):
                        around(d, s, part).start()
                    if part == 0:
                        sign = 1 if d == 0 else NZ - 1
                        owner = lax.rem(z + (NZ - sign) * s, NZ)
                        spread(owner)
                        fresh.append(owner)
        for owner in done:
            pass_on(owner)
        done = fresh
    for owner in done:
        pass_on(owner)

    @pl.loop(0, NZ)
    def _(owner):
        onward(owner).wait()
        across(0, owner).wait_send()
        across(1, owner).wait_send()

    for k in range(1, NY):
        over_y(k).wait_send()
    for d in range(2):
        for part in range(2):
            for s in range(steps(d, part)):
                around(d, s, part).wait_send()

    @pl.loop(0, NT)
    def _(tt):
        @pl.loop(0, 16)
        def _(pair):
            yy = pair // 4
            zz = lax.rem(pair, 4) * 2
            a = wg[yy, zz, tt].astype(F32)
            b = wg[yy, zz + 1, tt].astype(F32)
            rows = pl.ds(pl.multiple_of(pair * 48, 48), 48)
            wn[tt, rows, 0:WIDE] = jnp.concatenate([a[:BAND], b[:BAND]], axis=0).astype(BF)
            wn[tt, rows, WIDE:HALF] = jnp.concatenate([a[BAND:], b[BAND:]], axis=0).astype(BF)

    load.wait()

    @pl.loop(0, 3)
    def _(n):
        cols = pl.ds(pl.multiple_of(n * 256, 256), 256)
        total = jnp.dot(nv[0], wn[0, :, cols], preferred_element_type=F32)
        for tt in range(1, NT):
            total = total + jnp.dot(nv[tt], wn[tt, :, cols], preferred_element_type=F32)
        out[:, cols] = total.astype(BF)


def run_c(wb, nc):
    any_spec = pl.BlockSpec(memory_space=pl.ANY)
    vmem = pl.BlockSpec(memory_space=pltpu.VMEM)
    dma = pltpu.SemaphoreType.DMA
    return pl.pallas_call(
        kernel_c,
        name="weights_and_product",
        out_shape=jax.ShapeDtypeStruct((512, HALF), BF),
        in_specs=[vmem, any_spec],
        out_specs=vmem,
        scratch_shapes=[
            pltpu.VMEM((NY, NZ, NT, 2 * BAND, WIDE), BF),
            pltpu.VMEM((NT, HALF, HALF), BF),
            pltpu.VMEM((NT, 512, HALF), BF),
            dma((1,)), dma((1,)),
            dma((8,)), dma((8,)),
            dma((4,)), dma((4,)),
            dma((2, 4)), dma((2, 4)),
            dma((3, 8)), dma((3, 8)),
            dma((2, 4)), dma((2, 4)),
        ],
        compiler_params=pltpu.CompilerParams(
            collective_id=1, has_side_effects=True, vmem_limit_bytes=48 * 2**20
        ),
        cost_estimate=pl.CostEstimate(flops=2 * 512 * 6144 * 768, bytes_accessed=8 * 2**20, transcendentals=0),
    )(wb, nc)


def shards(
    saved_master,
    saved_first,
    saved_second,
    piece_columns,
    load_order,
    context,
    out_grad,
    next_context,
):
    def grouped(saved):
        return saved[0].reshape(4, 192, WIDE).transpose(1, 0, 2)

    tokens = lax.all_gather(next_context, "tensor")
    rx, gq = run_a(grouped(saved_master), grouped(saved_first), grouped(saved_second), context, out_grad)
    new_master, new_first, new_second, blocks = run_b(
        piece_columns[0], load_order[0], rx.reshape(32 * SROWS, WIDE), gq
    )
    activations = run_c(blocks, tokens)
    return (new_master, new_first, new_second, activations)


def solution(mesh):
    placed = (
        P("tensor", "dp", None),
        P("tensor", "dp", None),
        P("tensor", "dp", None),
        P("tensor", None),
        P("tensor", None),
        P("dp", "tensor"),
        P("dp", None),
        P("dp", "tensor"),
    )
    return jax.shard_map(
        shards,
        mesh=mesh,
        in_specs=placed,
        out_specs=(
            P(("tensor", "dp"), None),
            P(("tensor", "dp"), None),
            P(("tensor", "dp"), None),
            P("dp", "tensor"),
        ),
        check_vma=False,
    )
```

```python
import jax
import jax.numpy as jnp
from jax import lax
from jax.experimental import pallas as pl
from jax.experimental.pallas import tpu as pltpu
from jax.sharding import PartitionSpec as P

first_bias = 1.0 - 0.9**20
second_bias = 1.0 - 0.95**20

MESH = pl.DeviceIdType.MESH
BF = jnp.bfloat16
F32 = jnp.float32
NY, NZ = 4, 8
NT = 8
BAND = 24
WIDE = 384
GROUPS = 6
SROWS = 72
QUARTER = 1536
HALF = 768


def where_am_i():
    dp = lax.axis_index("dp")
    t = lax.axis_index("tensor")
    return dp, t, dp // NZ, lax.rem(dp, NZ)


def remote(src, dst, send, recv, device):
    return pltpu.make_async_remote_copy(
        src_ref=src, dst_ref=dst, send_sem=send, recv_sem=recv, device_id=device, device_id_type=MESH
    )


STAGGER = 2
PARTS = 3
VMEM_A = 60 * 2**20
VMEM_C = 117 * 2**19


def kernel_a(
    sm, sf, ss, ctx, og, nc, rx, gq, nv,
    st, flat, tx, mid, ty, cg, ct, oq, grad, zs, zr, tot, ysb, nraw, nsend,
    load_sem, loc_sem, st_s, st_r, sy_s, sy_r, cx_s, cx_r, og_s, og_r, ox_s, ox_r, om_s, om_r, rs_s, rs_r, ya_s, ya_r,
    ny_s, ny_r, nx_s, nx_r, nm_s, nm_r,
):
    dp, t, y, z = where_am_i()
    core = lax.rem(t, 2)
    mate = t + 1 - 2 * core

    loads = [pltpu.make_async_copy(src, st.at[a], load_sem.at[a]) for a, src in enumerate((sm, sf, ss))]
    for copy in loads:
        copy.start()
    own_ctx = pltpu.make_async_copy(ctx, cg.at[pl.ds(y * 256, 256)], loc_sem.at[0])
    own_og = pltpu.make_async_copy(
        og.at[:, pl.ds(y * QUARTER, QUARTER)], oq.at[pl.ds(y * 256, 256)], loc_sem.at[1]
    )
    tokens_in = pltpu.make_async_copy(nc, nraw, loc_sem.at[9])
    tokens_in.start()
    own_ctx.start()
    own_og.start()

    barrier = pltpu.get_barrier_semaphore()

    for k in range(1, NY):
        pl.semaphore_signal(
            barrier, inc=1, device_id=(lax.rem(y + k, NY) * NZ + z, t), device_id_type=MESH
        )
    for k in range(1, NZ):
        pl.semaphore_signal(
            barrier, inc=1, device_id=(y * NZ + lax.rem(z + k, NZ), t), device_id_type=MESH
        )
    for k in range(1, 4):
        pl.semaphore_signal(barrier, inc=1, device_id=(dp, lax.rem(t + 2 * k, NT)), device_id_type=MESH)
    pl.semaphore_signal(barrier, inc=1, device_id=(dp, mate), device_id_type=MESH)
    pl.semaphore_wait(barrier, NY - 1 + NZ - 1 + 3 + 1)

    def ctx_copy(k):
        to = lax.rem(y + k, NY)
        return remote(ctx, cg.at[pl.ds(y * 256, 256)], cx_s.at[k], cx_r.at[k], (to * NZ + z, t))

    def og_copy(k):
        to = lax.rem(y + k, NY)
        return remote(
            og.at[pl.ds(t * 32, 32), pl.ds(to * QUARTER, QUARTER)],
            oq.at[pl.ds(y * 256 + t * 32, 32)],
            og_s.at[k], og_r.at[k], (to * NZ + z, t),
        )

    def og_rows(k, tt):
        return oq.at[pl.ds(lax.rem(y + NY - k, NY) * 256 + tt * 32, 32)]

    def og_over_x(k, kx):
        piece = og_rows(k, t)
        return remote(piece, piece, ox_s.at[k, kx], ox_r.at[k, kx], (dp, lax.rem(t + 2 * kx, NT)))

    def og_to_mate(k, kx):
        piece = og_rows(k, lax.rem(t + NT - 2 * kx, NT))
        return remote(piece, piece, om_s.at[k, kx], om_r.at[k, kx], (dp, mate))

    for k in (2, 1, 3):
        og_copy(k).start()
        ctx_copy(k).start()

    def lanes(tt):
        return pl.ds(pl.multiple_of(tt * 128, 128), 128)

    def tokens_over_y(k):
        to = lax.rem(y + k, NY)
        return remote(
            nsend.at[to], nv.at[y, :, lanes(t)], ny_s.at[k], ny_r.at[k], (to * NZ + z, t)
        )

    def tokens_over_x(k):
        piece = nv.at[:, :, lanes(t)]
        return remote(piece, piece, nx_s.at[k], nx_r.at[k], (dp, lax.rem(t + 2 * k, NT)))

    def tokens_to_mate(k):
        piece = nv.at[:, :, lanes(lax.rem(t + NT - 2 * k, NT))]
        return remote(piece, piece, nm_s.at[k], nm_r.at[k], (dp, mate))

    own_tokens = pltpu.make_async_copy(nsend.at[y], nv.at[y, :, lanes(t)], loc_sem.at[10])
    tokens_in.wait()
    for yy in range(NY):
        c0 = yy * 192
        nsend[yy, 0:512, :] = nraw[:, c0 : c0 + 128]
        tail = nraw[:, c0 + 128 : c0 + 192]
        nsend[yy, 512:768, :] = jnp.concatenate([tail[:256], tail[256:]], axis=1)
    for k in (2, 1, 3):
        tokens_over_y(k).start()
    own_tokens.start()

    for copy in loads:
        copy.wait()

    def state_copy(k):
        to = lax.rem(z + k, NZ)
        return remote(tx.at[k], mid.at[z], st_s.at[k], st_r.at[k], (y * NZ + to, t))

    def build(k):
        for ky in range(NY):
            owner = lax.rem(y + ky, NY) * NZ + lax.rem(z + k, NZ)
            for a in range(3):
                for g in range(GROUPS):
                    row = ky * SROWS + a * BAND + 4 * g
                    flat[row : row + 4, :] = st[a, owner * GROUPS + g]
        return flat[...].astype(BF)

    for k in (4, 3, 5, 2, 6, 1, 7):
        tx[k] = build(k)
        state_copy(k).start()
    mid[z] = build(0)

    def state_over_y(k, pair):
        to = lax.rem(y + k, NY) * NZ + z
        return remote(ty.at[pair, k], rx.at[y * 4 + pair], sy_s.at[pair, k], sy_r.at[pair, k], (to, t))

    def state_local(pair):
        return pltpu.make_async_copy(ty.at[pair, 0], rx.at[y * 4 + pair], loc_sem.at[5 + pair])

    def pass_state(pair):
        low = mid[2 * pair].astype(F32)
        high = mid[2 * pair + 1].astype(F32)
        for k in (2, 1, 3, 0):
            rows = slice(k * SROWS, (k + 1) * SROWS)
            ty[pair, k] = jnp.concatenate([low[rows], high[rows]], axis=0).astype(BF)
            if k:
                state_over_y(k, pair).start()
            else:
                state_local(pair).start()

    for k in (1, 3, 2):
        og_copy(k).wait_recv()
        for kx in (2, 1, 3):
            og_over_x(k, kx).start()
        og_to_mate(k, 0).start()

    own_ctx.wait()
    own_og.wait()

    def turn(source):
        ct[:, pl.ds(source * 256, 256)] = cg[pl.ds(source * 256, 256), :].T

    turn(y)
    for k in (1, 3, 2):
        ctx_copy(k).wait_recv()
        turn(lax.rem(y + NY - k, NY))
    for k in (1, 3, 2):
        for kx in (1, 3, 2):
            og_over_x(k, kx).wait_recv()
            og_to_mate(k, kx).start()
    for k in (1, 3, 2):
        for kx in range(4):
            og_to_mate(k, kx).wait_recv()

    def chunk(dest, h):
        return jnp.concatenate(
            [grad[pl.ds((yy * NZ + dest) * BAND, BAND), h * HALF : (h + 1) * HALF] for yy in range(NY)], axis=0
        )

    def steps(d, h):
        return 4 if d == h else 3

    def ring_copy(d, h, s):
        to = lax.rem(z + (1 if d == 0 else NZ - 1), NZ)
        return remote(zs.at[d, h, s], zr.at[d, h, s], rs_s.at[d, h, s], rs_r.at[d, h, s], (y * NZ + to, t))

    def ring_send(d, h, s):
        sign = 1 if d == 0 else NZ - 1
        dest = lax.rem(z + sign * (steps(d, h) - s), NZ)
        value = chunk(dest, h)
        if s > 0:
            ring_copy(d, h, s - 1).wait_recv()
            value = value + zr[d, h, s - 1].astype(F32)
        zs[d, h, s] = value.astype(BF)
        ring_copy(d, h, s).start()

    for h in range(2):
        @pl.loop(0, 3)
        def _(n):
            cols = pl.ds(h * HALF + n * 256, 256)
            grad[:, cols] = jnp.dot(ct[...], oq[:, cols], preferred_element_type=F32)

        ring_send(h, h, 0)
        ring_send(1 - h, h, 0)
        if h == 0:
            own_tokens.wait()
            for k in (1, 3, 2):
                tokens_over_y(k).wait_recv()
            for k in (2, 1, 3):
                tokens_over_x(k).start()
            tokens_to_mate(0).start()

    for s in range(1, 4):
        for h in range(2):
            for d in (h, 1 - h):
                if s < steps(d, h):
                    ring_send(d, h, s)
        if s == 1:
            for k in (1, 7, 2, 6, 3, 5, 4):
                state_copy(k).wait_recv()
        for pair in ((0, 1), (2, 3), ())[s - 1]:
            pass_state(pair)

    for k in (1, 3, 2):
        tokens_over_x(k).wait_recv()
        tokens_to_mate(k).start()

    def out_copy(k, h):
        to = lax.rem(y + k, NY)
        return remote(ysb.at[k, h], gq.at[y, h], ya_s.at[k, h], ya_r.at[k, h], (to * NZ + z, t))

    own_out = []
    for h in range(2):
        value = chunk(z, h)
        for d in (1 - h, h):
            last = steps(d, h) - 1
            ring_copy(d, h, last).wait_recv()
            value = value + zr[d, h, last].astype(F32)
        tot[...] = value
        for k in (2, 1, 3, 0):
            rows = pl.ds(lax.rem(y + k, NY) * BAND, BAND)
            ysb[k, h] = jnp.concatenate([tot[rows, 0:WIDE], tot[rows, WIDE:HALF]], axis=0).astype(BF)
            if k:
                out_copy(k, h).start()
            else:
                own_out.append(pltpu.make_async_copy(ysb.at[0, h], gq.at[y, h], loc_sem.at[3 + h]))
                own_out[-1].start()

    for k in (1, 2, 3):
        og_copy(k).wait_send()
        ctx_copy(k).wait_send()
        for kx in (1, 2, 3):
            og_over_x(k, kx).wait_send()
        for kx in range(4):
            og_to_mate(k, kx).wait_send()
    for h in range(2):
        for d in range(2):
            for s in range(steps(d, h)):
                ring_copy(d, h, s).wait_send()
        for k in (1, 2, 3):
            out_copy(k, h).wait()
        own_out[h].wait()
    for k in range(1, NZ):
        state_copy(k).wait_send()
    for k in range(1, 4):
        tokens_over_y(k).wait_send()
        tokens_over_x(k).wait_send()
    for k in range(4):
        tokens_to_mate(k).wait()
    for pair in range(4):
        for k in (1, 2, 3):
            state_over_y(k, pair).wait()
        state_local(pair).wait()


def run_a(sm, sf, ss, ctx, og, nc):
    hbm = pl.BlockSpec(memory_space=pltpu.HBM)
    dma = pltpu.SemaphoreType.DMA
    return pl.pallas_call(
        kernel_a,
        name="state_and_gradient",
        out_shape=(
            jax.ShapeDtypeStruct((16, 2 * SROWS, WIDE), BF),
            jax.ShapeDtypeStruct((NY, 2, 2 * BAND, WIDE), BF),
            jax.ShapeDtypeStruct((NY, 768, 1024), BF),
        ),
        in_specs=[hbm] * 6,
        out_specs=(hbm, hbm, hbm),
        scratch_shapes=[
            pltpu.VMEM((3, 192, 4, WIDE), F32),
            pltpu.VMEM((4 * SROWS, WIDE), F32),
            pltpu.VMEM((NZ, 4 * SROWS, WIDE), BF),
            pltpu.VMEM((NZ, 4 * SROWS, WIDE), BF),
            pltpu.VMEM((4, NY, 2 * SROWS, WIDE), BF),
            pltpu.VMEM((1024, HALF), BF),
            pltpu.VMEM((HALF, 1024), BF),
            pltpu.VMEM((1024, QUARTER), BF),
            pltpu.VMEM((HALF, QUARTER), F32),
            pltpu.VMEM((2, 2, 4, 4 * BAND, HALF), BF),
            pltpu.VMEM((2, 2, 4, 4 * BAND, HALF), BF),
            pltpu.VMEM((4 * BAND, HALF), F32),
            pltpu.VMEM((4, 2, 2 * BAND, WIDE), BF),
            pltpu.VMEM((512, HALF), BF),
            pltpu.VMEM((NY, 768, 128), BF),
            dma((3,)), dma((11,)),
            dma((8,)), dma((8,)),
            dma((4, 4)), dma((4, 4)),
            dma((4,)), dma((4,)), dma((4,)), dma((4,)),
            dma((4, 4)), dma((4, 4)), dma((4, 4)), dma((4, 4)),
            dma((2, 2, 4)), dma((2, 2, 4)),
            dma((4, 2)), dma((4, 2)),
            dma((4,)), dma((4,)), dma((4,)), dma((4,)), dma((4,)), dma((4,)),
        ],
        compiler_params=pltpu.CompilerParams(
            collective_id=0, has_side_effects=True, vmem_limit_bytes=VMEM_A
        ),
        cost_estimate=pl.CostEstimate(flops=2 * 1024 * 768 * 1536, bytes_accessed=16 * 2**20, transcendentals=0),
    )(sm, sf, ss, ctx, og, nc)


def kernel_b(pc, lo, rx_in, gq_in, nm, nf, ns, wb, rx, gq, sem, zbuf, obuf, gbuf, mbuf, fbuf, sbuf, starts):
    gq_copy = pltpu.make_async_copy(gq_in, gq, sem.at[0])
    rx_copy = pltpu.make_async_copy(rx_in, rx, sem.at[1])
    gq_copy.start()
    rx_copy.start()
    row = lax.broadcasted_iota(jnp.int32, (WIDE, 512), 0)
    col = lax.broadcasted_iota(jnp.int32, (WIDE, 512), 1)
    spread = ((row == (col // 128) * 96 + lax.rem(col, 128)) & (lax.rem(col, 128) < 96)).astype(BF)

    def count(j, total):
        starts[j] = total
        return total + pc[j]

    lax.fori_loop(0, 128, count, jnp.int32(0))

    gq_copy.wait()
    for yy in range(NY):
        for h in range(2):
            block = gq[yy, h].astype(F32)
            for q in range(2):
                c0 = yy * QUARTER + h * HALF + q * WIDE
                for n in range(3):
                    gbuf[c0 // 128 + n, 0:BAND, :] = block[q * BAND : (q + 1) * BAND, n * 128 : (n + 1) * 128]

    rx_copy.wait()

    @pl.loop(0, 9)
    def _(i):
        rows = pl.ds(i * 256, 256)
        value = jnp.dot(rx[rows, :], spread, preferred_element_type=F32)
        for r in range(4):
            zbuf[r, rows, :] = value[:, r * 128 : (r + 1) * 128]

    lane = lax.broadcasted_iota(jnp.int32, (8, 128), 1)

    @pl.loop(0, 128, unroll=4)
    def _(i):
        rank = lo[i]
        start = starts[rank]
        length = pc[rank]
        tile = start // 128
        offset = lax.rem(start, 128)
        keep = (lane >= offset) & (lane < offset + length)
        spill = lane < offset + length - 128
        base = (i // 4) * SROWS + lax.rem(i, 4)
        for a in range(3):
            for r in range(4):
                value = zbuf[r, pl.ds(base + a * BAND, 8, stride=4), :]
                value = pltpu.roll(value, offset, 1)
                pltpu.store(obuf.at[a * 4 + r, tile], value, mask=keep)
                pltpu.store(obuf.at[a * 4 + r, tile + 1], value, mask=spill)

    @pl.loop(0, 48, unroll=4)
    def _(n):
        cols = pl.ds(pl.multiple_of(n * 128, 128), 128)
        for r in range(4):
            rows = pl.ds(r, 8, stride=4)
            gradient = gbuf[n, rows, :]
            first = 0.9 * obuf[4 + r, n] + 0.1 * gradient
            second = 0.95 * obuf[8 + r, n] + 0.05 * gradient * gradient
            master = obuf[r, n] - 0.01 * (first / first_bias) / (jnp.sqrt(second / second_bias) + 1e-08)
            mbuf[n, rows, :] = master
            fbuf[n, rows, :] = first
            sbuf[n, rows, :] = second
        nm[:, cols] = mbuf[n, 0:BAND, :]
        nf[:, cols] = fbuf[n, 0:BAND, :]
        ns[:, cols] = sbuf[n, 0:BAND, :]

    for n in range(PARTS):
        for t in range(NT):
            c0 = t * HALF + n * 256
            wb[n, t] = jnp.concatenate([nm[:, c0 : c0 + 128], nm[:, c0 + 128 : c0 + 256]], axis=0).astype(BF)


def run_b(pc, lo, rx, gq):
    smem = pl.BlockSpec(memory_space=pltpu.SMEM)
    vmem = pl.BlockSpec(memory_space=pltpu.VMEM)
    hbm = pl.BlockSpec(memory_space=pltpu.HBM)
    state = jax.ShapeDtypeStruct((BAND, 6144), F32)
    return pl.pallas_call(
        kernel_b,
        name="place_and_adam",
        out_shape=(state, state, state, jax.ShapeDtypeStruct((PARTS, NT, 2 * BAND, 128), BF)),
        in_specs=[smem, smem, hbm, hbm],
        out_specs=(vmem, vmem, vmem, vmem),
        scratch_shapes=[
            pltpu.VMEM((32 * SROWS, WIDE), BF),
            pltpu.VMEM((NY, 2, 2 * BAND, WIDE), BF),
            pltpu.SemaphoreType.DMA((2,)),
            pltpu.VMEM((4, 32 * SROWS + 32, 128), F32),
            pltpu.VMEM((12, 50, 8, 128), F32),
            pltpu.VMEM((48, 32, 128), F32),
            pltpu.VMEM((48, 32, 128), F32),
            pltpu.VMEM((48, 32, 128), F32),
            pltpu.VMEM((48, 32, 128), F32),
            pltpu.SMEM((128,), jnp.int32),
        ],
        compiler_params=pltpu.CompilerParams(vmem_limit_bytes=VMEM_A),
        cost_estimate=pl.CostEstimate(flops=10**9, bytes_accessed=5 * 2**20, transcendentals=0),
    )(pc, lo, rx, gq)


def kernel_c(
    wb, nc, out, wg, wa, wl, wh, nv, own, po, ro,
    nc_sem, own_sem, w1_s, w1_r, zz_s, zz_r, yo_s, yo_r,
):
    dp, t, y, z = where_am_i()
    load = pltpu.make_async_copy(nc, nv, nc_sem.at[0])
    load.start()
    own_in = pltpu.make_async_copy(wb.at[:, t], wg.at[:, z, t], own_sem.at[0])
    own_in.start()

    barrier = pltpu.get_barrier_semaphore()
    for k in range(1, NT):
        pl.semaphore_signal(barrier, inc=1, device_id=(dp, lax.rem(t + k, NT)), device_id_type=MESH)
    for k in range(1, NY):
        pl.semaphore_signal(
            barrier, inc=1, device_id=(lax.rem(y + k, NY) * NZ + z, t), device_id_type=MESH
        )
    for k in (1, NZ - 1):
        pl.semaphore_signal(
            barrier, inc=1, device_id=(y * NZ + lax.rem(z + k, NZ), t), device_id_type=MESH
        )
    pl.semaphore_wait(barrier, NT - 1 + NY - 1 + 2)

    def first_copy(k):
        to = lax.rem(t + k, NT)
        return remote(wb.at[:, to], wg.at[:, z, t], w1_s.at[k], w1_r.at[k], (dp, to))

    for k in range(1, NT):
        first_copy(k).start()
    wl[...] = jnp.zeros_like(wl)
    wh[...] = jnp.zeros_like(wh)
    own_in.wait()
    for k in range(1, NT):
        first_copy(k).wait()

    def steps(d, n):
        return 4 if d == n % 2 else 3

    def around(d, s, n):
        sign = 1 if d == 0 else NZ - 1
        owner = lax.rem(z + (NZ - sign) * s, NZ)
        piece = wg.at[n, owner]
        return remote(
            piece, piece, zz_s.at[d, s, n], zz_r.at[d, s, n], (y * NZ + lax.rem(z + sign, NZ), t)
        )

    def back(k, n):
        to = lax.rem(y + k, NY) * NZ + z
        return remote(po.at[n, k - 1], ro.at[n, k - 1], yo_s.at[k, n], yo_r.at[k, n], (to, t))

    def arrange(n):
        @pl.loop(0, NT)
        def _(tt):
            base = pl.multiple_of(tt * 128, 128)
            for pair in range(4):
                a = wg[n, 2 * pair, tt].astype(F32)
                b = wg[n, 2 * pair + 1, tt].astype(F32)
                for q in range(2):
                    rows = slice(q * BAND, (q + 1) * BAND)
                    cols = slice(q * 128, (q + 1) * 128)
                    both = jnp.concatenate([a[rows], b[rows]], axis=0).astype(BF)
                    if pair < 2:
                        wa[n, pl.ds(base + pair * 48, 48), cols] = both
                    elif pair == 2:
                        wa[n, pl.ds(base + 96, 32), cols] = both[:32]
                        wl[n, pl.ds(base, 16), cols] = both[32:]
                        wh[n, pl.ds(base + 64, 16), cols] = both[32:]
                    else:
                        wl[n, pl.ds(base + 16, 48), cols] = both
                        wh[n, pl.ds(base + 80, 48), cols] = both

    def multiply(n):
        for k in (2, 1, 3, 0):
            ys = lax.rem(y + k, NY)
            for half, tail in ((0, wl), (1, wh)):
                rows = slice(half * 256, (half + 1) * 256)
                value = jnp.dot(nv[ys, rows, :], wa[n], preferred_element_type=F32)
                value = value + jnp.dot(nv[ys, 512:768, :], tail[n], preferred_element_type=F32)
                if k:
                    po[n, k - 1, rows, :] = value.astype(BF)
                else:
                    own[n, rows, :] = value
            if k:
                back(k, n).start()

    for tick in range(5 + STAGGER * (PARTS - 1)):
        for n in range(PARTS):
            s = tick - STAGGER * n
            for d in range(2):
                if s > 0 and s - 1 < steps(d, n):
                    around(d, s - 1, n).wait_recv()
                if 0 <= s < steps(d, n):
                    around(d, s, n).start()
        for n in range(PARTS):
            if tick - STAGGER * n == 4:
                if n == 0:
                    load.wait()
                arrange(n)
                multiply(n)

    for n in range(PARTS):
        value = own[n]
        for k in (1, 3, 2):
            back(k, n).wait_recv()
            value = value + ro[n, k - 1].astype(F32)
        out[:, n * 256 : (n + 1) * 256] = value.astype(BF)

    for n in range(PARTS):
        for d in range(2):
            for s in range(steps(d, n)):
                around(d, s, n).wait_send()
        for k in range(1, NY):
            back(k, n).wait_send()


def run_c(wb, nc):
    hbm = pl.BlockSpec(memory_space=pltpu.HBM)
    vmem = pl.BlockSpec(memory_space=pltpu.VMEM)
    dma = pltpu.SemaphoreType.DMA
    return pl.pallas_call(
        kernel_c,
        name="weights_and_product",
        out_shape=jax.ShapeDtypeStruct((512, HALF), BF),
        in_specs=[hbm, hbm],
        out_specs=vmem,
        scratch_shapes=[
            pltpu.VMEM((PARTS, NZ, NT, 2 * BAND, 128), BF),
            pltpu.VMEM((PARTS, 1024, 256), BF),
            pltpu.VMEM((PARTS, 1024, 256), BF),
            pltpu.VMEM((PARTS, 1024, 256), BF),
            pltpu.VMEM((NY, 768, 1024), BF),
            pltpu.VMEM((PARTS, 512, 256), F32),
            pltpu.VMEM((PARTS, NY - 1, 512, 256), BF),
            pltpu.VMEM((PARTS, NY - 1, 512, 256), BF),
            dma((1,)), dma((1,)),
            dma((8,)), dma((8,)),
            dma((2, 4, PARTS)), dma((2, 4, PARTS)),
            dma((4, PARTS)), dma((4, PARTS)),
        ],
        compiler_params=pltpu.CompilerParams(
            collective_id=1, has_side_effects=True, vmem_limit_bytes=VMEM_C
        ),
        cost_estimate=pl.CostEstimate(flops=2 * 512 * 6144 * 768, bytes_accessed=8 * 2**20, transcendentals=0),
    )(wb, nc)


def shards(
    saved_master,
    saved_first,
    saved_second,
    piece_columns,
    load_order,
    context,
    out_grad,
    next_context,
):
    def grouped(saved):
        return saved[0].reshape(4, 192, WIDE).transpose(1, 0, 2)

    rx, gq, tokens = run_a(
        grouped(saved_master), grouped(saved_first), grouped(saved_second), context, out_grad, next_context
    )
    new_master, new_first, new_second, blocks = run_b(
        piece_columns[0], load_order[0], rx.reshape(32 * SROWS, WIDE), gq
    )
    activations = run_c(blocks, tokens)
    return (new_master, new_first, new_second, activations)


def solution(mesh):
    placed = (
        P("tensor", "dp", None),
        P("tensor", "dp", None),
        P("tensor", "dp", None),
        P("tensor", None),
        P("tensor", None),
        P("dp", "tensor"),
        P("dp", None),
        P("dp", "tensor"),
    )
    return jax.shard_map(
        shards,
        mesh=mesh,
        in_specs=placed,
        out_specs=(
            P(("tensor", "dp"), None),
            P(("tensor", "dp"), None),
            P(("tensor", "dp"), None),
            P("dp", "tensor"),
        ),
        check_vma=False,
    )
```

```python
import jax
import jax.numpy as jnp
from jax import lax
from jax.experimental import pallas as pl
from jax.experimental.pallas import tpu as pltpu
from jax.sharding import PartitionSpec as P

first_bias = 1.0 - 0.9**20
second_bias = 1.0 - 0.95**20

MESH = pl.DeviceIdType.MESH
BF = jnp.bfloat16
F32 = jnp.float32
NY, NZ = 4, 8
NT = 8
BAND = 24
WIDE = 384
GROUPS = 6
SROWS = 72
QUARTER = 1536
HALF = 768


def where_am_i():
    dp = lax.axis_index("dp")
    t = lax.axis_index("tensor")
    return dp, t, dp // NZ, lax.rem(dp, NZ)


def remote(src, dst, send, recv, device):
    return pltpu.make_async_remote_copy(
        src_ref=src, dst_ref=dst, send_sem=send, recv_sem=recv, device_id=device, device_id_type=MESH
    )


STAGGER = 2
PARTS = 3
VMEM_A = 60 * 2**20
VMEM_C = 104 * 2**19
VMEM_B = 125 * 2**19


def kernel_a(
    sm, sf, ss, ctx, og, nc, rx, gq, nv,
    st, flat, tx, mid, ty, cg, ct, oq, grad, zs, zr, tot, ysb, nraw, nsend,
    load_sem, loc_sem, st_s, st_r, sy_s, sy_r, cx_s, cx_r, og_s, og_r, ox_s, ox_r, om_s, om_r, rs_s, rs_r, ya_s, ya_r,
    ny_s, ny_r, nx_s, nx_r, nm_s, nm_r,
):
    dp, t, y, z = where_am_i()
    core = lax.rem(t, 2)
    mate = t + 1 - 2 * core

    loads = [pltpu.make_async_copy(src, st.at[a], load_sem.at[a]) for a, src in enumerate((sm, sf, ss))]
    for copy in loads:
        copy.start()
    own_ctx = pltpu.make_async_copy(ctx, cg.at[pl.ds(y * 256, 256)], loc_sem.at[0])
    own_og = pltpu.make_async_copy(
        og.at[:, pl.ds(y * QUARTER, QUARTER)], oq.at[pl.ds(y * 256, 256)], loc_sem.at[1]
    )
    tokens_in = pltpu.make_async_copy(nc, nraw, loc_sem.at[9])
    tokens_in.start()
    own_ctx.start()
    own_og.start()

    barrier = pltpu.get_barrier_semaphore()

    for k in range(1, NY):
        pl.semaphore_signal(
            barrier, inc=1, device_id=(lax.rem(y + k, NY) * NZ + z, t), device_id_type=MESH
        )
    for k in range(1, NZ):
        pl.semaphore_signal(
            barrier, inc=1, device_id=(y * NZ + lax.rem(z + k, NZ), t), device_id_type=MESH
        )
    for k in range(1, 4):
        pl.semaphore_signal(barrier, inc=1, device_id=(dp, lax.rem(t + 2 * k, NT)), device_id_type=MESH)
    pl.semaphore_signal(barrier, inc=1, device_id=(dp, mate), device_id_type=MESH)
    pl.semaphore_wait(barrier, NY - 1 + NZ - 1 + 3 + 1)

    def ctx_copy(k):
        to = lax.rem(y + k, NY)
        return remote(ctx, cg.at[pl.ds(y * 256, 256)], cx_s.at[k], cx_r.at[k], (to * NZ + z, t))

    def og_copy(k):
        to = lax.rem(y + k, NY)
        return remote(
            og.at[pl.ds(t * 32, 32), pl.ds(to * QUARTER, QUARTER)],
            oq.at[pl.ds(y * 256 + t * 32, 32)],
            og_s.at[k], og_r.at[k], (to * NZ + z, t),
        )

    def og_rows(k, tt):
        return oq.at[pl.ds(lax.rem(y + NY - k, NY) * 256 + tt * 32, 32)]

    def og_over_x(k, kx):
        piece = og_rows(k, t)
        return remote(piece, piece, ox_s.at[k, kx], ox_r.at[k, kx], (dp, lax.rem(t + 2 * kx, NT)))

    def og_to_mate(k, kx):
        piece = og_rows(k, lax.rem(t + NT - 2 * kx, NT))
        return remote(piece, piece, om_s.at[k, kx], om_r.at[k, kx], (dp, mate))

    for k in (2, 1, 3):
        og_copy(k).start()
        ctx_copy(k).start()

    def lanes(tt):
        return pl.ds(pl.multiple_of(tt * 128, 128), 128)

    def tokens_over_y(k):
        to = lax.rem(y + k, NY)
        return remote(
            nsend.at[to], nv.at[y, :, lanes(t)], ny_s.at[k], ny_r.at[k], (to * NZ + z, t)
        )

    def tokens_over_x(k):
        piece = nv.at[:, :, lanes(t)]
        return remote(piece, piece, nx_s.at[k], nx_r.at[k], (dp, lax.rem(t + 2 * k, NT)))

    def tokens_to_mate(k):
        piece = nv.at[:, :, lanes(lax.rem(t + NT - 2 * k, NT))]
        return remote(piece, piece, nm_s.at[k], nm_r.at[k], (dp, mate))

    own_tokens = pltpu.make_async_copy(nsend.at[y], nv.at[y, :, lanes(t)], loc_sem.at[10])
    tokens_in.wait()
    for yy in range(NY):
        c0 = yy * 192
        nsend[yy, 0:512, :] = nraw[:, c0 : c0 + 128]
        tail = nraw[:, c0 + 128 : c0 + 192]
        nsend[yy, 512:768, :] = jnp.concatenate([tail[:256], tail[256:]], axis=1)
    for k in (2, 1, 3):
        tokens_over_y(k).start()
    own_tokens.start()

    for copy in loads:
        copy.wait()

    def state_copy(k):
        to = lax.rem(z + k, NZ)
        return remote(tx.at[k], mid.at[z], st_s.at[k], st_r.at[k], (y * NZ + to, t))

    def build(k):
        for ky in range(NY):
            owner = lax.rem(y + ky, NY) * NZ + lax.rem(z + k, NZ)
            for a in range(3):
                for g in range(GROUPS):
                    row = ky * SROWS + a * BAND + 4 * g
                    flat[row : row + 4, :] = st[a, owner * GROUPS + g]
        return flat[...].astype(BF)

    for k in (4, 3, 5, 2, 6, 1, 7):
        tx[k] = build(k)
        state_copy(k).start()
    mid[z] = build(0)

    def state_over_y(k, pair):
        to = lax.rem(y + k, NY) * NZ + z
        return remote(ty.at[pair, k], rx.at[y * 4 + pair], sy_s.at[pair, k], sy_r.at[pair, k], (to, t))

    def state_local(pair):
        return pltpu.make_async_copy(ty.at[pair, 0], rx.at[y * 4 + pair], loc_sem.at[5 + pair])

    def pass_state(pair):
        low = mid[2 * pair].astype(F32)
        high = mid[2 * pair + 1].astype(F32)
        for k in (2, 1, 3, 0):
            rows = slice(k * SROWS, (k + 1) * SROWS)
            ty[pair, k] = jnp.concatenate([low[rows], high[rows]], axis=0).astype(BF)
            if k:
                state_over_y(k, pair).start()
            else:
                state_local(pair).start()

    for k in (1, 3, 2):
        og_copy(k).wait_recv()
        for kx in (2, 1, 3):
            og_over_x(k, kx).start()
        og_to_mate(k, 0).start()

    own_ctx.wait()
    own_og.wait()

    def turn(source):
        ct[:, pl.ds(source * 256, 256)] = cg[pl.ds(source * 256, 256), :].T

    turn(y)
    for k in (1, 3, 2):
        ctx_copy(k).wait_recv()
        turn(lax.rem(y + NY - k, NY))
    for k in (1, 3, 2):
        for kx in (1, 3, 2):
            og_over_x(k, kx).wait_recv()
            og_to_mate(k, kx).start()
    for k in (1, 3, 2):
        for kx in range(4):
            og_to_mate(k, kx).wait_recv()

    def chunk(dest, h):
        return jnp.concatenate(
            [grad[pl.ds((yy * NZ + dest) * BAND, BAND), h * HALF : (h + 1) * HALF] for yy in range(NY)], axis=0
        )

    def steps(d, h):
        return 4 if d == h else 3

    def ring_copy(d, h, s):
        to = lax.rem(z + (1 if d == 0 else NZ - 1), NZ)
        return remote(zs.at[d, h, s], zr.at[d, h, s], rs_s.at[d, h, s], rs_r.at[d, h, s], (y * NZ + to, t))

    def ring_send(d, h, s):
        sign = 1 if d == 0 else NZ - 1
        dest = lax.rem(z + sign * (steps(d, h) - s), NZ)
        value = chunk(dest, h)
        if s > 0:
            ring_copy(d, h, s - 1).wait_recv()
            value = value + zr[d, h, s - 1].astype(F32)
        zs[d, h, s] = value.astype(BF)
        ring_copy(d, h, s).start()

    for h in range(2):
        @pl.loop(0, 3)
        def _(n):
            cols = pl.ds(h * HALF + n * 256, 256)
            grad[:, cols] = jnp.dot(ct[...], oq[:, cols], preferred_element_type=F32)

        ring_send(h, h, 0)
        ring_send(1 - h, h, 0)
        if h == 0:
            own_tokens.wait()
            for k in (1, 3, 2):
                tokens_over_y(k).wait_recv()
            for k in (2, 1, 3):
                tokens_over_x(k).start()
            tokens_to_mate(0).start()

    for s in range(1, 4):
        for h in range(2):
            for d in (h, 1 - h):
                if s < steps(d, h):
                    ring_send(d, h, s)
        if s == 1:
            for k in (1, 7, 2, 6, 3, 5, 4):
                state_copy(k).wait_recv()
        for pair in ((0, 1), (2, 3), ())[s - 1]:
            pass_state(pair)

    for k in (1, 3, 2):
        tokens_over_x(k).wait_recv()
        tokens_to_mate(k).start()

    def out_copy(k, h):
        to = lax.rem(y + k, NY)
        return remote(ysb.at[k, h], gq.at[y, h], ya_s.at[k, h], ya_r.at[k, h], (to * NZ + z, t))

    own_out = []
    for h in range(2):
        value = chunk(z, h)
        for d in (1 - h, h):
            last = steps(d, h) - 1
            ring_copy(d, h, last).wait_recv()
            value = value + zr[d, h, last].astype(F32)
        tot[...] = value
        for k in (2, 1, 3, 0):
            rows = pl.ds(lax.rem(y + k, NY) * BAND, BAND)
            ysb[k, h] = jnp.concatenate([tot[rows, 0:WIDE], tot[rows, WIDE:HALF]], axis=0).astype(BF)
            if k:
                out_copy(k, h).start()
            else:
                own_out.append(pltpu.make_async_copy(ysb.at[0, h], gq.at[y, h], loc_sem.at[3 + h]))
                own_out[-1].start()

    for k in (1, 2, 3):
        og_copy(k).wait_send()
        ctx_copy(k).wait_send()
        for kx in (1, 2, 3):
            og_over_x(k, kx).wait_send()
        for kx in range(4):
            og_to_mate(k, kx).wait_send()
    for h in range(2):
        for d in range(2):
            for s in range(steps(d, h)):
                ring_copy(d, h, s).wait_send()
        for k in (1, 2, 3):
            out_copy(k, h).wait()
        own_out[h].wait()
    for k in range(1, NZ):
        state_copy(k).wait_send()
    for k in range(1, 4):
        tokens_over_y(k).wait_send()
        tokens_over_x(k).wait_send()
    for k in range(4):
        tokens_to_mate(k).wait()
    for pair in range(4):
        for k in (1, 2, 3):
            state_over_y(k, pair).wait()
        state_local(pair).wait()


def run_a(sm, sf, ss, ctx, og, nc):
    hbm = pl.BlockSpec(memory_space=pltpu.HBM)
    dma = pltpu.SemaphoreType.DMA
    return pl.pallas_call(
        kernel_a,
        name="state_and_gradient",
        out_shape=(
            jax.ShapeDtypeStruct((16, 2 * SROWS, WIDE), BF),
            jax.ShapeDtypeStruct((NY, 2, 2 * BAND, WIDE), BF),
            jax.ShapeDtypeStruct((NY, 768, 1024), BF),
        ),
        in_specs=[hbm] * 6,
        out_specs=(hbm, hbm, hbm),
        scratch_shapes=[
            pltpu.VMEM((3, 192, 4, WIDE), F32),
            pltpu.VMEM((4 * SROWS, WIDE), F32),
            pltpu.VMEM((NZ, 4 * SROWS, WIDE), BF),
            pltpu.VMEM((NZ, 4 * SROWS, WIDE), BF),
            pltpu.VMEM((4, NY, 2 * SROWS, WIDE), BF),
            pltpu.VMEM((1024, HALF), BF),
            pltpu.VMEM((HALF, 1024), BF),
            pltpu.VMEM((1024, QUARTER), BF),
            pltpu.VMEM((HALF, QUARTER), F32),
            pltpu.VMEM((2, 2, 4, 4 * BAND, HALF), BF),
            pltpu.VMEM((2, 2, 4, 4 * BAND, HALF), BF),
            pltpu.VMEM((4 * BAND, HALF), F32),
            pltpu.VMEM((4, 2, 2 * BAND, WIDE), BF),
            pltpu.VMEM((512, HALF), BF),
            pltpu.VMEM((NY, 768, 128), BF),
            dma((3,)), dma((11,)),
            dma((8,)), dma((8,)),
            dma((4, 4)), dma((4, 4)),
            dma((4,)), dma((4,)), dma((4,)), dma((4,)),
            dma((4, 4)), dma((4, 4)), dma((4, 4)), dma((4, 4)),
            dma((2, 2, 4)), dma((2, 2, 4)),
            dma((4, 2)), dma((4, 2)),
            dma((4,)), dma((4,)), dma((4,)), dma((4,)), dma((4,)), dma((4,)),
        ],
        compiler_params=pltpu.CompilerParams(
            collective_id=0, has_side_effects=True, vmem_limit_bytes=VMEM_A
        ),
        cost_estimate=pl.CostEstimate(flops=2 * 1024 * 768 * 1536, bytes_accessed=16 * 2**20, transcendentals=0),
    )(sm, sf, ss, ctx, og, nc)


def kernel_b(pc, lo, rx_in, gq_in, nm, nf, ns, wb, rx, gq, sem, zbuf, obuf, gbuf, mbuf, fbuf, sbuf, starts):
    gq_copy = pltpu.make_async_copy(gq_in, gq, sem.at[0])
    rx_copy = pltpu.make_async_copy(rx_in, rx, sem.at[1])
    gq_copy.start()
    rx_copy.start()
    row = lax.broadcasted_iota(jnp.int32, (WIDE, 512), 0)
    col = lax.broadcasted_iota(jnp.int32, (WIDE, 512), 1)
    spread = ((row == (col // 128) * 96 + lax.rem(col, 128)) & (lax.rem(col, 128) < 96)).astype(BF)

    def count(j, total):
        starts[j] = total
        return total + pc[j]

    lax.fori_loop(0, 128, count, jnp.int32(0))

    gq_copy.wait()
    for yy in range(NY):
        for h in range(2):
            block = gq[yy, h].astype(F32)
            for q in range(2):
                c0 = yy * QUARTER + h * HALF + q * WIDE
                for n in range(3):
                    gbuf[c0 // 128 + n, 0:BAND, :] = block[q * BAND : (q + 1) * BAND, n * 128 : (n + 1) * 128]

    rx_copy.wait()

    @pl.loop(0, 9)
    def _(i):
        rows = pl.ds(i * 256, 256)
        value = jnp.dot(rx[rows, :], spread, preferred_element_type=F32)
        for r in range(4):
            zbuf[r, rows, :] = value[:, r * 128 : (r + 1) * 128]

    lane = lax.broadcasted_iota(jnp.int32, (8, 128), 1)

    @pl.loop(0, 128, unroll=4)
    def _(i):
        rank = lo[i]
        start = starts[rank]
        length = pc[rank]
        tile = start // 128
        offset = lax.rem(start, 128)
        keep = (lane >= offset) & (lane < offset + length)
        spill = lane < offset + length - 128
        base = (i // 4) * SROWS + lax.rem(i, 4)
        for a in range(3):
            for r in range(4):
                value = zbuf[r, pl.ds(base + a * BAND, 8, stride=4), :]
                value = pltpu.roll(value, offset, 1)
                pltpu.store(obuf.at[a * 4 + r, tile], value, mask=keep)
                pltpu.store(obuf.at[a * 4 + r, tile + 1], value, mask=spill)

    @pl.loop(0, 48, unroll=4)
    def _(n):
        cols = pl.ds(pl.multiple_of(n * 128, 128), 128)
        for r in range(4):
            rows = pl.ds(r, 8, stride=4)
            gradient = gbuf[n, rows, :]
            first = 0.9 * obuf[4 + r, n] + 0.1 * gradient
            second = 0.95 * obuf[8 + r, n] + 0.05 * gradient * gradient
            master = obuf[r, n] - 0.01 * (first / first_bias) / (jnp.sqrt(second / second_bias) + 1e-08)
            mbuf[n, rows, :] = master
            fbuf[n, rows, :] = first
            sbuf[n, rows, :] = second
        nm[:, cols] = mbuf[n, 0:BAND, :]
        nf[:, cols] = fbuf[n, 0:BAND, :]
        ns[:, cols] = sbuf[n, 0:BAND, :]

    for n in range(PARTS):
        for t in range(NT):
            c0 = t * HALF + n * 256
            wb[n, t] = jnp.concatenate([nm[:, c0 : c0 + 128], nm[:, c0 + 128 : c0 + 256]], axis=0).astype(BF)


def run_b(pc, lo, rx, gq):
    smem = pl.BlockSpec(memory_space=pltpu.SMEM)
    vmem = pl.BlockSpec(memory_space=pltpu.VMEM)
    hbm = pl.BlockSpec(memory_space=pltpu.HBM)
    state = jax.ShapeDtypeStruct((BAND, 6144), F32)
    return pl.pallas_call(
        kernel_b,
        name="place_and_adam",
        out_shape=(state, state, state, jax.ShapeDtypeStruct((PARTS, NT, 2 * BAND, 128), BF)),
        in_specs=[smem, smem, hbm, hbm],
        out_specs=(vmem, vmem, vmem, vmem),
        scratch_shapes=[
            pltpu.VMEM((32 * SROWS, WIDE), BF),
            pltpu.VMEM((NY, 2, 2 * BAND, WIDE), BF),
            pltpu.SemaphoreType.DMA((2,)),
            pltpu.VMEM((4, 32 * SROWS + 32, 128), F32),
            pltpu.VMEM((12, 50, 8, 128), F32),
            pltpu.VMEM((48, 32, 128), F32),
            pltpu.VMEM((48, 32, 128), F32),
            pltpu.VMEM((48, 32, 128), F32),
            pltpu.VMEM((48, 32, 128), F32),
            pltpu.SMEM((128,), jnp.int32),
        ],
        compiler_params=pltpu.CompilerParams(vmem_limit_bytes=VMEM_B),
        cost_estimate=pl.CostEstimate(flops=10**9, bytes_accessed=5 * 2**20, transcendentals=0),
    )(pc, lo, rx, gq)


def kernel_c(
    wb, nc, out, wg, wa, wl, wh, nv, own, held, po, ro,
    nc_sem, own_sem, w1_s, w1_r, zz_s, zz_r, yo_s, yo_r,
):
    dp, t, y, z = where_am_i()
    load = pltpu.make_async_copy(nc, nv, nc_sem.at[0])
    load.start()
    own_in = pltpu.make_async_copy(wb.at[:, t], wg.at[:, z, t], own_sem.at[0])
    own_in.start()

    barrier = pltpu.get_barrier_semaphore()
    for k in range(1, NT):
        pl.semaphore_signal(barrier, inc=1, device_id=(dp, lax.rem(t + k, NT)), device_id_type=MESH)
    for k in range(1, NY):
        pl.semaphore_signal(
            barrier, inc=1, device_id=(lax.rem(y + k, NY) * NZ + z, t), device_id_type=MESH
        )
    for k in (1, NZ - 1):
        pl.semaphore_signal(
            barrier, inc=1, device_id=(y * NZ + lax.rem(z + k, NZ), t), device_id_type=MESH
        )
    pl.semaphore_wait(barrier, NT - 1 + NY - 1 + 2)

    def first_copy(k, n):
        to = lax.rem(t + k, NT)
        return remote(wb.at[n, to], wg.at[n, z, t], w1_s.at[k, n], w1_r.at[k, n], (dp, to))

    for n in range(PARTS):
        for k in range(1, NT):
            first_copy(k, n).start()
    wl[...] = jnp.zeros_like(wl)
    wh[...] = jnp.zeros_like(wh)
    own_in.wait()

    def steps(d, n):
        return 4 if d == n % 2 else 3

    def around(d, s, n, part):
        sign = 1 if d == 0 else NZ - 1
        owner = lax.rem(z + (NZ - sign) * s, NZ)
        piece = wg.at[n, owner, pl.ds(part * 4, 4)]
        return remote(
            piece, piece, zz_s.at[d, s, n, part], zz_r.at[d, s, n, part],
            (y * NZ + lax.rem(z + sign, NZ), t),
        )

    def back(kind, n):
        to = lax.rem(y + (1 if kind % 2 == 0 else NY - 1), NY) * NZ + z
        return remote(po.at[n, kind], ro.at[n, kind], yo_s.at[kind, n], yo_r.at[kind, n], (to, t))

    def arrange(n):
        @pl.loop(0, NT)
        def _(tt):
            base = pl.multiple_of(tt * 128, 128)
            for pair in range(4):
                a = wg[n, 2 * pair, tt].astype(F32)
                b = wg[n, 2 * pair + 1, tt].astype(F32)
                for q in range(2):
                    rows = slice(q * BAND, (q + 1) * BAND)
                    cols = slice(q * 128, (q + 1) * 128)
                    both = jnp.concatenate([a[rows], b[rows]], axis=0).astype(BF)
                    if pair < 2:
                        wa[n, pl.ds(base + pair * 48, 48), cols] = both
                    elif pair == 2:
                        wa[n, pl.ds(base + 96, 32), cols] = both[:32]
                        wl[n, pl.ds(base, 16), cols] = both[32:]
                        wh[n, pl.ds(base + 64, 16), cols] = both[32:]
                    else:
                        wl[n, pl.ds(base + 16, 48), cols] = both
                        wh[n, pl.ds(base + 80, 48), cols] = both

    def product(n, k, half):
        ys = lax.rem(y + k, NY)
        value = jnp.dot(nv[ys, half * 256 : half * 256 + 256, :], wa[n], preferred_element_type=F32)
        tail = (wl, wh)[half]
        return value + jnp.dot(nv[ys, 512:768, :], tail[n], preferred_element_type=F32)

    def multiply(n):
        for kind, k, half in ((0, 2, 0), (1, 2, 1), (2, 1, 1), (3, 3, 0)):
            po[n, kind] = product(n, k, half).astype(BF)
            back(kind, n).start()
        held[n, 0] = product(n, 1, 0)
        held[n, 1] = product(n, 3, 1)
        own[n, 0:256, :] = product(n, 0, 0)
        own[n, 256:512, :] = product(n, 0, 1)

    def join(n):
        for d in range(2):
            back(d, n).wait_recv()
            po[n, 4 + d] = (held[n, d] + ro[n, d].astype(F32)).astype(BF)
            back(4 + d, n).start()

    for tick in range(6 + STAGGER * (PARTS - 1)):
        for n in range(PARTS):
            s = tick - STAGGER * n
            if s == 0:
                for k in range(1, NT):
                    first_copy(k, n).wait_recv()
            for part in range(2):
                for d in range(2):
                    if s > 0 and s - 1 < steps(d, n):
                        around(d, s - 1, n, part).wait_recv()
                    if 0 <= s < steps(d, n):
                        around(d, s, n, part).start()
        for n in range(PARTS):
            if tick - STAGGER * n == 4:
                if n == 0:
                    load.wait()
                arrange(n)
                multiply(n)
            if tick - STAGGER * n == 5:
                join(n)

    for n in range(PARTS):
        cols = slice(n * 256, (n + 1) * 256)
        for half, kinds in ((0, (3, 4)), (1, (2, 5))):
            rows = slice(half * 256, half * 256 + 256)
            value = own[n, rows, :]
            for kind in kinds:
                back(kind, n).wait_recv()
                value = value + ro[n, kind].astype(F32)
            out[rows, cols] = value.astype(BF)

    for n in range(PARTS):
        for k in range(1, NT):
            first_copy(k, n).wait_send()
        for d in range(2):
            for s in range(steps(d, n)):
                for part in range(2):
                    around(d, s, n, part).wait_send()
        for kind in range(6):
            back(kind, n).wait_send()


def run_c(wb, nc):
    hbm = pl.BlockSpec(memory_space=pltpu.HBM)
    vmem = pl.BlockSpec(memory_space=pltpu.VMEM)
    dma = pltpu.SemaphoreType.DMA
    return pl.pallas_call(
        kernel_c,
        name="weights_and_product",
        out_shape=jax.ShapeDtypeStruct((512, HALF), BF),
        in_specs=[hbm, hbm],
        out_specs=vmem,
        scratch_shapes=[
            pltpu.VMEM((PARTS, NZ, NT, 2 * BAND, 128), BF),
            pltpu.VMEM((PARTS, 1024, 256), BF),
            pltpu.VMEM((PARTS, 1024, 256), BF),
            pltpu.VMEM((PARTS, 1024, 256), BF),
            pltpu.VMEM((NY, 768, 1024), BF),
            pltpu.VMEM((PARTS, 512, 256), F32),
            pltpu.VMEM((PARTS, 2, 256, 256), F32),
            pltpu.VMEM((PARTS, 6, 256, 256), BF),
            pltpu.VMEM((PARTS, 6, 256, 256), BF),
            dma((1,)), dma((1,)),
            dma((8, PARTS)), dma((8, PARTS)),
            dma((2, 4, PARTS, 2)), dma((2, 4, PARTS, 2)),
            dma((6, PARTS)), dma((6, PARTS)),
        ],
        compiler_params=pltpu.CompilerParams(
            collective_id=1, has_side_effects=True, vmem_limit_bytes=VMEM_C
        ),
        cost_estimate=pl.CostEstimate(flops=2 * 512 * 6144 * 768, bytes_accessed=8 * 2**20, transcendentals=0),
    )(wb, nc)


def shards(
    saved_master,
    saved_first,
    saved_second,
    piece_columns,
    load_order,
    context,
    out_grad,
    next_context,
):
    def grouped(saved):
        return saved[0].reshape(4, 192, WIDE).transpose(1, 0, 2)

    rx, gq, tokens = run_a(
        grouped(saved_master), grouped(saved_first), grouped(saved_second), context, out_grad, next_context
    )
    new_master, new_first, new_second, blocks = run_b(
        piece_columns[0], load_order[0], rx.reshape(32 * SROWS, WIDE), gq
    )
    activations = run_c(blocks, tokens)
    return (new_master, new_first, new_second, activations)


def solution(mesh):
    placed = (
        P("tensor", "dp", None),
        P("tensor", "dp", None),
        P("tensor", "dp", None),
        P("tensor", None),
        P("tensor", None),
        P("dp", "tensor"),
        P("dp", None),
        P("dp", "tensor"),
    )
    return jax.shard_map(
        shards,
        mesh=mesh,
        in_specs=placed,
        out_specs=(
            P(("tensor", "dp"), None),
            P(("tensor", "dp"), None),
            P(("tensor", "dp"), None),
            P("dp", "tensor"),
        ),
        check_vma=False,
    )
```

```python
import jax
import jax.numpy as jnp
from jax import lax
from jax.experimental import pallas as pl
from jax.experimental.pallas import tpu as pltpu
from jax.sharding import PartitionSpec as P

first_bias = 1.0 - 0.9**20
second_bias = 1.0 - 0.95**20

MESH = pl.DeviceIdType.MESH
BF = jnp.bfloat16
F32 = jnp.float32
NY, NZ = 4, 8
NT = 8
BAND = 24
WIDE = 384
GROUPS = 6
SROWS = 72
QUARTER = 1536
HALF = 768


def where_am_i():
    dp = lax.axis_index("dp")
    t = lax.axis_index("tensor")
    return dp, t, dp // NZ, lax.rem(dp, NZ)


def remote(src, dst, send, recv, device):
    return pltpu.make_async_remote_copy(
        src_ref=src, dst_ref=dst, send_sem=send, recv_sem=recv, device_id=device, device_id_type=MESH
    )


SUBS = (4, 2, 2)
STAGGER = 2
ROOM = 32
PARTS = 3
VMEM_A = 60 * 2**20
VMEM_C = 104 * 2**19
VMEM_B = 60 * 2**20


def kernel_a(
    sm, sf, ss, ctx, og, nc, rx, gq, nv,
    st, flat, tx, mid, ty, cg, ct, oq, grad, zs, zr, tot, ysb, nraw, nsend,
    load_sem, loc_sem, st_s, st_r, sy_s, sy_r, cx_s, cx_r, og_s, og_r, ox_s, ox_r, om_s, om_r, rs_s, rs_r, ya_s, ya_r,
    ny_s, ny_r, nx_s, nx_r, nm_s, nm_r,
):
    dp, t, y, z = where_am_i()
    core = lax.rem(t, 2)
    mate = t + 1 - 2 * core

    loads = [pltpu.make_async_copy(src, st.at[a], load_sem.at[a]) for a, src in enumerate((sm, sf, ss))]
    for copy in loads:
        copy.start()
    own_ctx = pltpu.make_async_copy(ctx, cg.at[pl.ds(y * 256, 256)], loc_sem.at[0])
    own_og = pltpu.make_async_copy(
        og.at[:, pl.ds(y * QUARTER, QUARTER)], oq.at[pl.ds(y * 256, 256)], loc_sem.at[1]
    )
    tokens_in = pltpu.make_async_copy(nc, nraw, loc_sem.at[9])
    tokens_in.start()
    own_ctx.start()
    own_og.start()

    barrier = pltpu.get_barrier_semaphore()

    for k in range(1, NY):
        pl.semaphore_signal(
            barrier, inc=1, device_id=(lax.rem(y + k, NY) * NZ + z, t), device_id_type=MESH
        )
    for k in range(1, NZ):
        pl.semaphore_signal(
            barrier, inc=1, device_id=(y * NZ + lax.rem(z + k, NZ), t), device_id_type=MESH
        )
    for k in range(1, 4):
        pl.semaphore_signal(barrier, inc=1, device_id=(dp, lax.rem(t + 2 * k, NT)), device_id_type=MESH)
    pl.semaphore_signal(barrier, inc=1, device_id=(dp, mate), device_id_type=MESH)
    pl.semaphore_wait(barrier, NY - 1 + NZ - 1 + 3 + 1)

    def ctx_copy(k):
        to = lax.rem(y + k, NY)
        return remote(ctx, cg.at[pl.ds(y * 256, 256)], cx_s.at[k], cx_r.at[k], (to * NZ + z, t))

    def og_copy(k):
        to = lax.rem(y + k, NY)
        return remote(
            og.at[pl.ds(t * 32, 32), pl.ds(to * QUARTER, QUARTER)],
            oq.at[pl.ds(y * 256 + t * 32, 32)],
            og_s.at[k], og_r.at[k], (to * NZ + z, t),
        )

    def og_rows(k, tt):
        return oq.at[pl.ds(lax.rem(y + NY - k, NY) * 256 + tt * 32, 32)]

    def og_over_x(k, kx):
        piece = og_rows(k, t)
        return remote(piece, piece, ox_s.at[k, kx], ox_r.at[k, kx], (dp, lax.rem(t + 2 * kx, NT)))

    def og_to_mate(k, kx):
        piece = og_rows(k, lax.rem(t + NT - 2 * kx, NT))
        return remote(piece, piece, om_s.at[k, kx], om_r.at[k, kx], (dp, mate))

    def lanes(tt):
        return pl.ds(pl.multiple_of(tt * 128, 128), 128)

    def tokens_over_y(k):
        to = lax.rem(y + k, NY)
        return remote(
            nsend.at[to], nv.at[y, :, lanes(t)], ny_s.at[k], ny_r.at[k], (to * NZ + z, t)
        )

    def tokens_over_x(k):
        piece = nv.at[:, :, lanes(t)]
        return remote(piece, piece, nx_s.at[k], nx_r.at[k], (dp, lax.rem(t + 2 * k, NT)))

    def tokens_to_mate(k):
        piece = nv.at[:, :, lanes(lax.rem(t + NT - 2 * k, NT))]
        return remote(piece, piece, nm_s.at[k], nm_r.at[k], (dp, mate))

    for k in (2, 1, 3):
        og_copy(k).start()
    own_tokens = pltpu.make_async_copy(nsend.at[y], nv.at[y, :, lanes(t)], loc_sem.at[10])
    tokens_in.wait()
    for yy in range(NY):
        c0 = yy * 192
        nsend[yy, 0:512, :] = nraw[:, c0 : c0 + 128]
        tail = nraw[:, c0 + 128 : c0 + 192]
        nsend[yy, 512:768, :] = jnp.concatenate([tail[:256], tail[256:]], axis=1)
    for k in (2, 1, 3):
        tokens_over_y(k).start()
    own_tokens.start()
    for k in (2, 1, 3):
        ctx_copy(k).start()

    for copy in loads:
        copy.wait()

    def state_copy(k):
        to = lax.rem(z + k, NZ)
        return remote(tx.at[k], mid.at[k], st_s.at[k], st_r.at[k], (y * NZ + to, t))

    def build(k):
        for ky in range(NY):
            owner = lax.rem(y + ky, NY) * NZ + lax.rem(z + k, NZ)
            for a in range(3):
                for g in range(GROUPS):
                    row = ky * SROWS + a * BAND + 4 * g
                    flat[row : row + 4, :] = st[a, owner * GROUPS + g]
        return flat[...].astype(BF)

    for k in (4, 3, 5, 2, 6, 1, 7):
        tx[k] = build(k)
        state_copy(k).start()
    mid[0] = build(0)

    def state_over_y(k, pair):
        to = lax.rem(y + k, NY) * NZ + z
        return remote(ty.at[pair, k], rx.at[y * 4 + pair], sy_s.at[pair, k], sy_r.at[pair, k], (to, t))

    def state_local(pair):
        return pltpu.make_async_copy(ty.at[pair, 0], rx.at[y * 4 + pair], loc_sem.at[5 + pair])

    def pass_state(pair):
        first, second = ((0, 4), (3, 5), (2, 6), (1, 7))[pair]
        if first:
            state_copy(first).wait_recv()
        state_copy(second).wait_recv()
        low = mid[first].astype(F32)
        high = mid[second].astype(F32)
        for k in (2, 1, 3, 0):
            rows = slice(k * SROWS, (k + 1) * SROWS)
            ty[pair, k] = jnp.concatenate([low[rows], high[rows]], axis=0).astype(BF)
            if k:
                state_over_y(k, pair).start()
            else:
                state_local(pair).start()

    for k in (1, 3, 2):
        og_copy(k).wait_recv()
        for kx in (2, 1, 3):
            og_over_x(k, kx).start()
        og_to_mate(k, 0).start()
    own_tokens.wait()
    for k in (1, 3, 2):
        tokens_over_y(k).wait_recv()
    for k in (2, 1, 3):
        tokens_over_x(k).start()
    tokens_to_mate(0).start()

    own_ctx.wait()
    own_og.wait()

    def turn(source):
        ct[:, pl.ds(source * 256, 256)] = cg[pl.ds(source * 256, 256), :].T

    turn(y)
    for k in (1, 3, 2):
        ctx_copy(k).wait_recv()
        turn(lax.rem(y + NY - k, NY))
    for k in (1, 3, 2):
        for kx in (1, 3, 2):
            og_over_x(k, kx).wait_recv()
            og_to_mate(k, kx).start()
    for k in (1, 3, 2):
        for kx in range(4):
            og_to_mate(k, kx).wait_recv()

    def chunk(dest, h):
        return jnp.concatenate(
            [grad[pl.ds((yy * NZ + dest) * BAND, BAND), h * HALF : (h + 1) * HALF] for yy in range(NY)], axis=0
        )

    def steps(d, h):
        return 4 if d == h else 3

    def ring_copy(d, h, s):
        to = lax.rem(z + (1 if d == 0 else NZ - 1), NZ)
        return remote(zs.at[d, h, s], zr.at[d, h, s], rs_s.at[d, h, s], rs_r.at[d, h, s], (y * NZ + to, t))

    def ring_send(d, h, s):
        sign = 1 if d == 0 else NZ - 1
        dest = lax.rem(z + sign * (steps(d, h) - s), NZ)
        value = chunk(dest, h)
        if s > 0:
            ring_copy(d, h, s - 1).wait_recv()
            value = value + zr[d, h, s - 1].astype(F32)
        zs[d, h, s] = value.astype(BF)
        ring_copy(d, h, s).start()

    for h in range(2):
        @pl.loop(0, 3)
        def _(n):
            cols = pl.ds(h * HALF + n * 256, 256)
            grad[:, cols] = jnp.dot(ct[...], oq[:, cols], preferred_element_type=F32)

        ring_send(h, h, 0)
        ring_send(1 - h, h, 0)

    pass_state(0)
    for s in range(1, 4):
        for h in range(2):
            for d in (h, 1 - h):
                if s < steps(d, h):
                    ring_send(d, h, s)
        for pair in ((1, 2), (3,), ())[s - 1]:
            pass_state(pair)

    for k in (1, 3, 2):
        tokens_over_x(k).wait_recv()
        tokens_to_mate(k).start()

    def out_copy(k, h):
        to = lax.rem(y + k, NY)
        return remote(ysb.at[k, h], gq.at[y, h], ya_s.at[k, h], ya_r.at[k, h], (to * NZ + z, t))

    own_out = []
    for h in range(2):
        value = chunk(z, h)
        for d in (1 - h, h):
            last = steps(d, h) - 1
            ring_copy(d, h, last).wait_recv()
            value = value + zr[d, h, last].astype(F32)
        tot[...] = value
        for k in (2, 1, 3, 0):
            rows = pl.ds(lax.rem(y + k, NY) * BAND, BAND)
            ysb[k, h] = jnp.concatenate([tot[rows, 0:WIDE], tot[rows, WIDE:HALF]], axis=0).astype(BF)
            if k:
                out_copy(k, h).start()
            else:
                own_out.append(pltpu.make_async_copy(ysb.at[0, h], gq.at[y, h], loc_sem.at[3 + h]))
                own_out[-1].start()

    for k in (1, 2, 3):
        og_copy(k).wait_send()
        ctx_copy(k).wait_send()
        for kx in (1, 2, 3):
            og_over_x(k, kx).wait_send()
        for kx in range(4):
            og_to_mate(k, kx).wait_send()
    for h in range(2):
        for d in range(2):
            for s in range(steps(d, h)):
                ring_copy(d, h, s).wait_send()
        for k in (1, 2, 3):
            out_copy(k, h).wait()
        own_out[h].wait()
    for k in range(1, NZ):
        state_copy(k).wait_send()
    for k in range(1, 4):
        tokens_over_y(k).wait_send()
        tokens_over_x(k).wait_send()
    for k in range(4):
        tokens_to_mate(k).wait()
    for pair in range(4):
        for k in (1, 2, 3):
            state_over_y(k, pair).wait()
        state_local(pair).wait()


def run_a(sm, sf, ss, ctx, og, nc):
    hbm = pl.BlockSpec(memory_space=pltpu.HBM)
    dma = pltpu.SemaphoreType.DMA
    return pl.pallas_call(
        kernel_a,
        name="state_and_gradient",
        out_shape=(
            jax.ShapeDtypeStruct((16, 2 * SROWS, WIDE), BF),
            jax.ShapeDtypeStruct((NY, 2, 2 * BAND, WIDE), BF),
            jax.ShapeDtypeStruct((NY, 768, 1024), BF),
        ),
        in_specs=[hbm] * 6,
        out_specs=(hbm, hbm, hbm),
        scratch_shapes=[
            pltpu.VMEM((3, 192, 4, WIDE), F32),
            pltpu.VMEM((4 * SROWS, WIDE), F32),
            pltpu.VMEM((NZ, 4 * SROWS, WIDE), BF),
            pltpu.VMEM((NZ, 4 * SROWS, WIDE), BF),
            pltpu.VMEM((4, NY, 2 * SROWS, WIDE), BF),
            pltpu.VMEM((1024, HALF), BF),
            pltpu.VMEM((HALF, 1024), BF),
            pltpu.VMEM((1024, QUARTER), BF),
            pltpu.VMEM((HALF, QUARTER), F32),
            pltpu.VMEM((2, 2, 4, 4 * BAND, HALF), BF),
            pltpu.VMEM((2, 2, 4, 4 * BAND, HALF), BF),
            pltpu.VMEM((4 * BAND, HALF), F32),
            pltpu.VMEM((4, 2, 2 * BAND, WIDE), BF),
            pltpu.VMEM((512, HALF), BF),
            pltpu.VMEM((NY, 768, 128), BF),
            dma((3,)), dma((11,)),
            dma((8,)), dma((8,)),
            dma((4, 4)), dma((4, 4)),
            dma((4,)), dma((4,)), dma((4,)), dma((4,)),
            dma((4, 4)), dma((4, 4)), dma((4, 4)), dma((4, 4)),
            dma((2, 2, 4)), dma((2, 2, 4)),
            dma((4, 2)), dma((4, 2)),
            dma((4,)), dma((4,)), dma((4,)), dma((4,)), dma((4,)), dma((4,)),
        ],
        compiler_params=pltpu.CompilerParams(
            collective_id=0, has_side_effects=True, vmem_limit_bytes=VMEM_A
        ),
        cost_estimate=pl.CostEstimate(flops=2 * 1024 * 768 * 1536, bytes_accessed=16 * 2**20, transcendentals=0),
    )(sm, sf, ss, ctx, og, nc)


def kernel_b(pc_in, lo_in, rx_in, gq_in, nm, nf, ns, wb_out, pc, lo, wb, rx, gq, vm, vf, vs, sem, out_sem, zbuf, obuf, gbuf, mbuf, fbuf, sbuf, starts):
    gq_copy = pltpu.make_async_copy(gq_in, gq, sem.at[0])
    rx_copies = [
        pltpu.make_async_copy(rx_in.at[pl.ds(i * 576, 576)], rx.at[pl.ds(i * 576, 576)], sem.at[1 + i])
        for i in range(4)
    ]
    small = [
        pltpu.make_async_copy(src, dst, sem.at[5 + i]) for i, (src, dst) in enumerate(((pc_in, pc), (lo_in, lo)))
    ]
    for copy in small:
        copy.start()
    gq_copy.start()
    for copy in rx_copies:
        copy.start()

    z = lax.rem(lax.axis_index("dp"), NZ)

    def count(j, total):
        starts[j] = total
        return total + pc[j]

    for copy in small:
        copy.wait()
    lax.fori_loop(0, 128, count, jnp.int32(0))

    gq_copy.wait()
    for yy in range(NY):
        for h in range(2):
            block = gq[yy, h].astype(F32)
            for q in range(2):
                c0 = yy * QUARTER + h * HALF + q * WIDE
                for n in range(3):
                    gbuf[c0 // 128 + n, 0:BAND, :] = block[q * BAND : (q + 1) * BAND, n * 128 : (n + 1) * 128]

    for i in range(4):
        rx_copies[i].wait()

        @pl.loop(i * 4, i * 4 + 4, unroll=2)
        def _(i):
            rows = pl.ds(i * 144, 144)
            value = rx[rows, :].astype(F32)
            for tile in range(3):
                zbuf[tile, rows, :] = value[:, tile * 128 : (tile + 1) * 128]

    lane = lax.broadcasted_iota(jnp.int32, (8, 128), 1)

    @pl.loop(0, 128, unroll=8)
    def _(i):
        rank = lo[i]
        start = starts[rank]
        length = pc[rank]
        tile = start // 128
        offset = lax.rem(start, 128)
        keep = (lane >= offset) & (lane < offset + length)
        spill = lane < offset + length - 128
        k = lax.rem(z + NZ - lax.rem(i // 4, NZ), NZ)
        far = k // 4
        pair = lax.rem(NY + (2 * far - 1) * k, NY)
        slot = (i // 32) * NZ + 2 * pair + far
        base = slot * SROWS + lax.rem(i, 4)
        for a in range(3):
            low, middle, high = (zbuf[tile, pl.ds(base + a * BAND, 8, stride=4), :] for tile in range(3))
            for r, value in enumerate(
                (low, jnp.where(lane >= 96, low, middle), jnp.where(lane >= 64, middle, high), high)
            ):
                value = pltpu.roll(value, lax.rem(offset + 32 * r, 128), 1)
                pltpu.store(obuf.at[a * 4 + r, tile], value, mask=keep)
                pltpu.store(obuf.at[a * 4 + r, tile + 1], value, mask=spill)

    def results(t):
        cols = pl.ds(pl.multiple_of(t * HALF, HALF), HALF)
        return [
            pltpu.make_async_copy(src.at[:, cols], dst.at[:, cols], out_sem.at[a, t])
            for a, (src, dst) in enumerate(((vm, nm), (vf, nf), (vs, ns)))
        ]

    @pl.loop(0, NT)
    def _(t):
        for c in range(6):
            n = t * 6 + c
            cols = pl.ds(pl.multiple_of(n * 128, 128), 128)
            for r in range(4):
                rows = pl.ds(r, 8, stride=4)
                gradient = gbuf[n, rows, :]
                first = 0.9 * obuf[4 + r, n] + 0.1 * gradient
                second = 0.95 * obuf[8 + r, n] + 0.05 * gradient * gradient
                master = obuf[r, n] - 0.01 * (first / first_bias) / (jnp.sqrt(second / second_bias) + 1e-08)
                mbuf[n, rows, :] = master
                fbuf[n, rows, :] = first
                sbuf[n, rows, :] = second
            vm[:, cols] = mbuf[n, 0:BAND, :]
            vf[:, cols] = fbuf[n, 0:BAND, :]
            vs[:, cols] = sbuf[n, 0:BAND, :]
        for copy in results(t):
            copy.start()
        for part in range(PARTS):
            wb[part, t] = jnp.concatenate(
                [mbuf[t * 6 + 2 * part, 0:BAND, :], mbuf[t * 6 + 2 * part + 1, 0:BAND, :]], axis=0
            ).astype(BF)

    weights = pltpu.make_async_copy(wb, wb_out.at[pl.ds(0, PARTS)], sem.at[7])
    weights.start()
    for t in range(NT):
        for copy in results(t):
            copy.wait()
    weights.wait()


def run_b(pc, lo, rx, gq):
    hbm = pl.BlockSpec(memory_space=pltpu.HBM)
    state = jax.ShapeDtypeStruct((BAND, 6144), F32)
    return pl.pallas_call(
        kernel_b,
        name="place_and_adam",
        out_shape=(state, state, state, jax.ShapeDtypeStruct((ROOM, NT, 2 * BAND, 128), BF)),
        in_specs=[hbm, hbm, hbm, hbm],
        out_specs=(hbm, hbm, hbm, hbm),
        scratch_shapes=[
            pltpu.SMEM((128,), jnp.int32),
            pltpu.SMEM((128,), jnp.int32),
            pltpu.VMEM((PARTS, NT, 2 * BAND, 128), BF),
            pltpu.VMEM((32 * SROWS, WIDE), BF),
            pltpu.VMEM((NY, 2, 2 * BAND, WIDE), BF),
            pltpu.VMEM((BAND, 6144), F32),
            pltpu.VMEM((BAND, 6144), F32),
            pltpu.VMEM((BAND, 6144), F32),
            pltpu.SemaphoreType.DMA((8,)),
            pltpu.SemaphoreType.DMA((3, NT)),
            pltpu.VMEM((3, 32 * SROWS + 32, 128), F32),
            pltpu.VMEM((12, 50, 8, 128), F32),
            pltpu.VMEM((48, 32, 128), F32),
            pltpu.VMEM((48, 32, 128), F32),
            pltpu.VMEM((48, 32, 128), F32),
            pltpu.VMEM((48, 32, 128), F32),
            pltpu.SMEM((128,), jnp.int32),
        ],
        compiler_params=pltpu.CompilerParams(vmem_limit_bytes=VMEM_B),
        cost_estimate=pl.CostEstimate(flops=10**9, bytes_accessed=5 * 2**20, transcendentals=0),
    )(pc, lo, rx, gq)


def kernel_c(
    wb, nc, out, wg, wa, wl, wh, nv, own, held, po, ro,
    nc_sem, own_sem, w1_s, w1_r, zz_s, zz_r, yo_s, yo_r,
):
    dp, t, y, z = where_am_i()
    load = pltpu.make_async_copy(nc, nv, nc_sem.at[0])
    load.start()
    own_in = pltpu.make_async_copy(wb.at[pl.ds(0, PARTS), t], wg.at[:, z, t], own_sem.at[0])
    own_in.start()

    barrier = pltpu.get_barrier_semaphore()
    for k in range(1, NT):
        pl.semaphore_signal(barrier, inc=1, device_id=(dp, lax.rem(t + k, NT)), device_id_type=MESH)
    for k in range(1, NY):
        pl.semaphore_signal(
            barrier, inc=1, device_id=(lax.rem(y + k, NY) * NZ + z, t), device_id_type=MESH
        )
    for k in (1, NZ - 1):
        pl.semaphore_signal(
            barrier, inc=1, device_id=(y * NZ + lax.rem(z + k, NZ), t), device_id_type=MESH
        )
    pl.semaphore_wait(barrier, NT - 1 + NY - 1 + 2)

    def first_copy(k, n):
        to = lax.rem(t + k, NT)
        return remote(wb.at[n, to], wg.at[n, z, t], w1_s.at[k, n], w1_r.at[k, n], (dp, to))

    for n in range(PARTS):
        for k in range(1, NT):
            first_copy(k, n).start()
    wl[...] = jnp.zeros_like(wl)
    wh[...] = jnp.zeros_like(wh)
    own_in.wait()

    def steps(d, part):
        return 4 if d == part % 2 else 3

    def around(d, s, n, part):
        sign = 1 if d == 0 else NZ - 1
        owner = lax.rem(z + (NZ - sign) * s, NZ)
        width = NT // SUBS[n]
        piece = wg.at[n, owner, pl.ds(part * width, width)]
        return remote(
            piece, piece, zz_s.at[d, s, n, part], zz_r.at[d, s, n, part],
            (y * NZ + lax.rem(z + sign, NZ), t),
        )

    def back(kind, n):
        to = lax.rem(y + (1 if kind % 2 == 0 else NY - 1), NY) * NZ + z
        return remote(po.at[n, kind], ro.at[n, kind], yo_s.at[kind, n], yo_r.at[kind, n], (to, t))

    def arrange(n):
        @pl.loop(0, NT)
        def _(tt):
            base = pl.multiple_of(tt * 128, 128)
            for pair in range(4):
                a = wg[n, 2 * pair, tt].astype(F32)
                b = wg[n, 2 * pair + 1, tt].astype(F32)
                for q in range(2):
                    rows = slice(q * BAND, (q + 1) * BAND)
                    cols = slice(q * 128, (q + 1) * 128)
                    both = jnp.concatenate([a[rows], b[rows]], axis=0).astype(BF)
                    if pair < 2:
                        wa[n, pl.ds(base + pair * 48, 48), cols] = both
                    elif pair == 2:
                        wa[n, pl.ds(base + 96, 32), cols] = both[:32]
                        wl[n, pl.ds(base, 16), cols] = both[32:]
                        wh[n, pl.ds(base + 64, 16), cols] = both[32:]
                    else:
                        wl[n, pl.ds(base + 16, 48), cols] = both
                        wh[n, pl.ds(base + 80, 48), cols] = both

    def product(n, k, half):
        ys = lax.rem(y + k, NY)
        value = jnp.dot(nv[ys, half * 256 : half * 256 + 256, :], wa[n], preferred_element_type=F32)
        tail = (wl, wh)[half]
        return value + jnp.dot(nv[ys, 512:768, :], tail[n], preferred_element_type=F32)

    def multiply(n):
        for kind, k, half in ((0, 2, 0), (1, 2, 1), (2, 1, 1), (3, 3, 0)):
            po[n, kind] = product(n, k, half).astype(BF)
            back(kind, n).start()
        held[n, 0] = product(n, 1, 0)
        held[n, 1] = product(n, 3, 1)
        own[n, 0:256, :] = product(n, 0, 0)
        own[n, 256:512, :] = product(n, 0, 1)

    def join(n):
        for d in range(2):
            back(d, n).wait_recv()
            po[n, 4 + d] = (held[n, d] + ro[n, d].astype(F32)).astype(BF)
            back(4 + d, n).start()

    for tick in range(6 + STAGGER * (PARTS - 1)):
        for n in range(PARTS):
            s = tick - STAGGER * n
            if s == 0:
                for k in range(1, NT):
                    first_copy(k, n).wait_recv()
            for part in range(SUBS[n]):
                for d in range(2):
                    if s > 0 and s - 1 < steps(d, part):
                        around(d, s - 1, n, part).wait_recv()
                    if 0 <= s < steps(d, part):
                        around(d, s, n, part).start()
        for n in range(PARTS):
            if tick - STAGGER * n == 4:
                if n == 0:
                    load.wait()
                arrange(n)
                multiply(n)
            if tick - STAGGER * n == 5:
                join(n)

    for n in range(PARTS):
        cols = slice(n * 256, (n + 1) * 256)
        for half, kinds in ((0, (3, 4)), (1, (2, 5))):
            rows = slice(half * 256, half * 256 + 256)
            value = own[n, rows, :]
            for kind in kinds:
                back(kind, n).wait_recv()
                value = value + ro[n, kind].astype(F32)
            out[rows, cols] = value.astype(BF)

    for n in range(PARTS):
        for k in range(1, NT):
            first_copy(k, n).wait_send()
        for d in range(2):
            for part in range(SUBS[n]):
                for s in range(steps(d, part)):
                    around(d, s, n, part).wait_send()
        for kind in range(6):
            back(kind, n).wait_send()


def run_c(wb, nc):
    hbm = pl.BlockSpec(memory_space=pltpu.HBM)
    vmem = pl.BlockSpec(memory_space=pltpu.VMEM)
    dma = pltpu.SemaphoreType.DMA
    return pl.pallas_call(
        kernel_c,
        name="weights_and_product",
        out_shape=jax.ShapeDtypeStruct((512, HALF), BF),
        in_specs=[hbm, hbm],
        out_specs=vmem,
        scratch_shapes=[
            pltpu.VMEM((PARTS, NZ, NT, 2 * BAND, 128), BF),
            pltpu.VMEM((PARTS, 1024, 256), BF),
            pltpu.VMEM((PARTS, 1024, 256), BF),
            pltpu.VMEM((PARTS, 1024, 256), BF),
            pltpu.VMEM((NY, 768, 1024), BF),
            pltpu.VMEM((PARTS, 512, 256), F32),
            pltpu.VMEM((PARTS, 2, 256, 256), F32),
            pltpu.VMEM((PARTS, 6, 256, 256), BF),
            pltpu.VMEM((PARTS, 6, 256, 256), BF),
            dma((1,)), dma((1,)),
            dma((8, PARTS)), dma((8, PARTS)),
            dma((2, 4, PARTS, 4)), dma((2, 4, PARTS, 4)),
            dma((6, PARTS)), dma((6, PARTS)),
        ],
        compiler_params=pltpu.CompilerParams(
            collective_id=1, has_side_effects=True, vmem_limit_bytes=VMEM_C
        ),
        cost_estimate=pl.CostEstimate(flops=2 * 512 * 6144 * 768, bytes_accessed=8 * 2**20, transcendentals=0),
    )(wb, nc)


def shards(
    saved_master,
    saved_first,
    saved_second,
    piece_columns,
    load_order,
    context,
    out_grad,
    next_context,
):
    def grouped(saved):
        return saved[0].reshape(4, 192, WIDE).transpose(1, 0, 2)

    rx, gq, tokens = run_a(
        grouped(saved_master), grouped(saved_first), grouped(saved_second), context, out_grad, next_context
    )
    new_master, new_first, new_second, blocks = run_b(
        piece_columns[0], load_order[0], rx.reshape(32 * SROWS, WIDE), gq
    )
    activations = run_c(blocks, tokens)
    return (new_master, new_first, new_second, activations)


def solution(mesh):
    placed = (
        P("tensor", "dp", None),
        P("tensor", "dp", None),
        P("tensor", "dp", None),
        P("tensor", None),
        P("tensor", None),
        P("dp", "tensor"),
        P("dp", None),
        P("dp", "tensor"),
    )
    return jax.shard_map(
        shards,
        mesh=mesh,
        in_specs=placed,
        out_specs=(
            P(("tensor", "dp"), None),
            P(("tensor", "dp"), None),
            P(("tensor", "dp"), None),
            P("dp", "tensor"),
        ),
        check_vma=False,
    )
```

```python
import jax
import jax.numpy as jnp
from jax import lax
from jax.experimental import pallas as pl
from jax.experimental.pallas import tpu as pltpu
from jax.sharding import PartitionSpec as P

first_bias = 1.0 - 0.9**20
second_bias = 1.0 - 0.95**20

MESH = pl.DeviceIdType.MESH
BF = jnp.bfloat16
F32 = jnp.float32
NY, NZ = 4, 8
NT = 8
BAND = 24
WIDE = 384
GROUPS = 6
SROWS = 72
QUARTER = 1536
HALF = 768


def where_am_i():
    dp = lax.axis_index("dp")
    t = lax.axis_index("tensor")
    return dp, t, dp // NZ, lax.rem(dp, NZ)


def remote(src, dst, send, recv, device):
    return pltpu.make_async_remote_copy(
        src_ref=src, dst_ref=dst, send_sem=send, recv_sem=recv, device_id=device, device_id_type=MESH
    )


SUBS = (4, 2, 2)
STAGGER = 2
ROOM = 32
PARTS = 3
VMEM_A = 60 * 2**20
VMEM_C = 104 * 2**19
VMEM_B = 60 * 2**20


def kernel_a(
    sm, sf, ss, ctx, og, nc, rx, gq, nv,
    st, flat, tx, mid, ty, cg, ct, oq, grad, zs, zr, tot, ysb, nraw, nsend,
    load_sem, loc_sem, st_s, st_r, sy_s, sy_r, cx_s, cx_r, og_s, og_r, ox_s, ox_r, om_s, om_r, rs_s, rs_r, ya_s, ya_r,
    ny_s, ny_r, nx_s, nx_r, nm_s, nm_r,
):
    dp, t, y, z = where_am_i()
    core = lax.rem(t, 2)
    mate = t + 1 - 2 * core

    loads = [pltpu.make_async_copy(src, st.at[a], load_sem.at[a]) for a, src in enumerate((sm, sf, ss))]
    for copy in loads:
        copy.start()
    own_ctx = pltpu.make_async_copy(ctx, cg.at[pl.ds(y * 256, 256)], loc_sem.at[0])
    own_og = pltpu.make_async_copy(
        og.at[:, pl.ds(y * QUARTER, QUARTER)], oq.at[pl.ds(y * 256, 256)], loc_sem.at[1]
    )
    tokens_in = pltpu.make_async_copy(nc, nraw, loc_sem.at[9])
    tokens_in.start()
    own_ctx.start()
    own_og.start()

    barrier = pltpu.get_barrier_semaphore()

    for k in range(1, NY):
        pl.semaphore_signal(
            barrier, inc=1, device_id=(lax.rem(y + k, NY) * NZ + z, t), device_id_type=MESH
        )
    for k in range(1, NZ):
        pl.semaphore_signal(
            barrier, inc=1, device_id=(y * NZ + lax.rem(z + k, NZ), t), device_id_type=MESH
        )
    for k in range(1, 4):
        pl.semaphore_signal(barrier, inc=1, device_id=(dp, lax.rem(t + 2 * k, NT)), device_id_type=MESH)
    pl.semaphore_signal(barrier, inc=1, device_id=(dp, mate), device_id_type=MESH)
    pl.semaphore_wait(barrier, NY - 1 + NZ - 1 + 3 + 1)

    def ctx_copy(k):
        to = lax.rem(y + k, NY)
        return remote(ctx, cg.at[pl.ds(y * 256, 256)], cx_s.at[k], cx_r.at[k], (to * NZ + z, t))

    def og_copy(k):
        to = lax.rem(y + k, NY)
        return remote(
            og.at[pl.ds(t * 32, 32), pl.ds(to * QUARTER, QUARTER)],
            oq.at[pl.ds(y * 256 + t * 32, 32)],
            og_s.at[k], og_r.at[k], (to * NZ + z, t),
        )

    def og_rows(k, tt):
        return oq.at[pl.ds(lax.rem(y + NY - k, NY) * 256 + tt * 32, 32)]

    def og_over_x(k, kx):
        piece = og_rows(k, t)
        return remote(piece, piece, ox_s.at[k, kx], ox_r.at[k, kx], (dp, lax.rem(t + 2 * kx, NT)))

    def og_to_mate(k, kx):
        piece = og_rows(k, lax.rem(t + NT - 2 * kx, NT))
        return remote(piece, piece, om_s.at[k, kx], om_r.at[k, kx], (dp, mate))

    def lanes(tt):
        return pl.ds(pl.multiple_of(tt * 128, 128), 128)

    def tokens_over_y(k):
        to = lax.rem(y + k, NY)
        return remote(
            nsend.at[to], nv.at[y, :, lanes(t)], ny_s.at[k], ny_r.at[k], (to * NZ + z, t)
        )

    def tokens_over_x(k, kx):
        piece = nv.at[lax.rem(y + NY - k, NY), :, lanes(t)]
        return remote(
            piece if k else nsend.at[y], piece, nx_s.at[k, kx], nx_r.at[k, kx], (dp, lax.rem(t + 2 * kx, NT))
        )

    def tokens_to_mate(k, kx):
        piece = nv.at[lax.rem(y + NY - k, NY), :, lanes(lax.rem(t + NT - 2 * kx, NT))]
        return remote(
            piece if k or kx else nsend.at[y], piece, nm_s.at[k, kx], nm_r.at[k, kx], (dp, mate)
        )

    def tokens_onward(k):
        for kx in (2, 1, 3):
            tokens_over_x(k, kx).start()
        tokens_to_mate(k, 0).start()

    def tokens_passed(k):
        for kx in (1, 3, 2):
            tokens_over_x(k, kx).wait_recv()
            tokens_to_mate(k, kx).start()

    for k in (2, 1, 3):
        og_copy(k).start()
    own_tokens = pltpu.make_async_copy(nsend.at[y], nv.at[y, :, lanes(t)], loc_sem.at[10])
    tokens_in.wait()
    for yy in range(NY):
        c0 = yy * 192
        nsend[yy, 0:512, :] = nraw[:, c0 : c0 + 128]
        tail = nraw[:, c0 + 128 : c0 + 192]
        nsend[yy, 512:768, :] = jnp.concatenate([tail[:256], tail[256:]], axis=1)
    for k in (2, 1, 3):
        tokens_over_y(k).start()
    own_tokens.start()
    tokens_onward(0)
    for k in (2, 1, 3):
        ctx_copy(k).start()

    for copy in loads:
        copy.wait()

    def state_copy(k):
        to = lax.rem(z + k, NZ)
        return remote(tx.at[k], mid.at[k], st_s.at[k], st_r.at[k], (y * NZ + to, t))

    def build(k):
        for ky in range(NY):
            owner = lax.rem(y + ky, NY) * NZ + lax.rem(z + k, NZ)
            for a in range(3):
                for g in range(GROUPS):
                    row = ky * SROWS + a * BAND + 4 * g
                    flat[row : row + 4, :] = st[a, owner * GROUPS + g]
        return flat[...].astype(BF)

    for k in (4, 3, 5, 2, 6, 1, 7):
        tx[k] = build(k)
        state_copy(k).start()
    mid[0] = build(0)

    def state_over_y(k, pair):
        to = lax.rem(y + k, NY) * NZ + z
        return remote(ty.at[pair, k], rx.at[y * 4 + pair], sy_s.at[pair, k], sy_r.at[pair, k], (to, t))

    def state_local(pair):
        return pltpu.make_async_copy(ty.at[pair, 0], rx.at[y * 4 + pair], loc_sem.at[5 + pair])

    def pass_state(pair):
        first, second = ((0, 4), (3, 5), (2, 6), (1, 7))[pair]
        if first:
            state_copy(first).wait_recv()
        state_copy(second).wait_recv()
        low = mid[first].astype(F32)
        high = mid[second].astype(F32)
        for k in (2, 1, 3, 0):
            rows = slice(k * SROWS, (k + 1) * SROWS)
            ty[pair, k] = jnp.concatenate([low[rows], high[rows]], axis=0).astype(BF)
            if k:
                state_over_y(k, pair).start()
            else:
                state_local(pair).start()

    for k in (1, 3, 2):
        og_copy(k).wait_recv()
        for kx in (2, 1, 3):
            og_over_x(k, kx).start()
        og_to_mate(k, 0).start()
    for k in (1, 3, 2):
        tokens_over_y(k).wait_recv()
        tokens_onward(k)

    own_ctx.wait()
    own_og.wait()

    def turn(source):
        ct[:, pl.ds(source * 256, 256)] = cg[pl.ds(source * 256, 256), :].T

    turn(y)
    for k in (1, 3, 2):
        ctx_copy(k).wait_recv()
        turn(lax.rem(y + NY - k, NY))
    for k in (1, 3, 2):
        for kx in (1, 3, 2):
            og_over_x(k, kx).wait_recv()
            og_to_mate(k, kx).start()
    for k in (1, 3, 2):
        for kx in range(4):
            og_to_mate(k, kx).wait_recv()

    def chunk(dest, h):
        return jnp.concatenate(
            [grad[pl.ds((yy * NZ + dest) * BAND, BAND), h * HALF : (h + 1) * HALF] for yy in range(NY)], axis=0
        )

    def steps(d, h):
        return 4 if d == h else 3

    def ring_copy(d, h, s):
        to = lax.rem(z + (1 if d == 0 else NZ - 1), NZ)
        return remote(zs.at[d, h, s], zr.at[d, h, s], rs_s.at[d, h, s], rs_r.at[d, h, s], (y * NZ + to, t))

    def ring_send(d, h, s):
        sign = 1 if d == 0 else NZ - 1
        dest = lax.rem(z + sign * (steps(d, h) - s), NZ)
        value = chunk(dest, h)
        if s > 0:
            ring_copy(d, h, s - 1).wait_recv()
            value = value + zr[d, h, s - 1].astype(F32)
        zs[d, h, s] = value.astype(BF)
        ring_copy(d, h, s).start()

    for h in range(2):
        @pl.loop(0, 3)
        def _(n):
            cols = pl.ds(h * HALF + n * 256, 256)
            grad[:, cols] = jnp.dot(ct[...], oq[:, cols], preferred_element_type=F32)

        ring_send(h, h, 0)
        ring_send(1 - h, h, 0)

    pass_state(0)
    tokens_passed(0)
    for s in range(1, 4):
        for h in range(2):
            for d in (h, 1 - h):
                if s < steps(d, h):
                    ring_send(d, h, s)
        for pair in ((1, 2), (3,), ())[s - 1]:
            pass_state(pair)
        for k in ((), (1,), (3,))[s - 1]:
            tokens_passed(k)

    tokens_passed(2)

    def out_copy(k, h):
        to = lax.rem(y + k, NY)
        return remote(ysb.at[k, h], gq.at[y, h], ya_s.at[k, h], ya_r.at[k, h], (to * NZ + z, t))

    own_out = []
    for h in range(2):
        value = chunk(z, h)
        for d in (1 - h, h):
            last = steps(d, h) - 1
            ring_copy(d, h, last).wait_recv()
            value = value + zr[d, h, last].astype(F32)
        tot[...] = value
        for k in (2, 1, 3, 0):
            rows = pl.ds(lax.rem(y + k, NY) * BAND, BAND)
            ysb[k, h] = jnp.concatenate([tot[rows, 0:WIDE], tot[rows, WIDE:HALF]], axis=0).astype(BF)
            if k:
                out_copy(k, h).start()
            else:
                own_out.append(pltpu.make_async_copy(ysb.at[0, h], gq.at[y, h], loc_sem.at[3 + h]))
                own_out[-1].start()

    for k in (1, 2, 3):
        og_copy(k).wait_send()
        ctx_copy(k).wait_send()
        for kx in (1, 2, 3):
            og_over_x(k, kx).wait_send()
        for kx in range(4):
            og_to_mate(k, kx).wait_send()
    for h in range(2):
        for d in range(2):
            for s in range(steps(d, h)):
                ring_copy(d, h, s).wait_send()
        for k in (1, 2, 3):
            out_copy(k, h).wait()
        own_out[h].wait()
    for k in range(1, NZ):
        state_copy(k).wait_send()
    for k in range(1, 4):
        tokens_over_y(k).wait_send()
    own_tokens.wait()
    for k in range(4):
        for kx in range(1, 4):
            tokens_over_x(k, kx).wait_send()
        for kx in range(4):
            tokens_to_mate(k, kx).wait()
    for pair in range(4):
        for k in (1, 2, 3):
            state_over_y(k, pair).wait()
        state_local(pair).wait()


def run_a(sm, sf, ss, ctx, og, nc):
    hbm = pl.BlockSpec(memory_space=pltpu.HBM)
    dma = pltpu.SemaphoreType.DMA
    return pl.pallas_call(
        kernel_a,
        name="state_and_gradient",
        out_shape=(
            jax.ShapeDtypeStruct((16, 2 * SROWS, WIDE), BF),
            jax.ShapeDtypeStruct((NY, 2, 2 * BAND, WIDE), BF),
            jax.ShapeDtypeStruct((NY, 768, 1024), BF),
        ),
        in_specs=[hbm] * 6,
        out_specs=(hbm, hbm, hbm),
        scratch_shapes=[
            pltpu.VMEM((3, 192, 4, WIDE), F32),
            pltpu.VMEM((4 * SROWS, WIDE), F32),
            pltpu.VMEM((NZ, 4 * SROWS, WIDE), BF),
            pltpu.VMEM((NZ, 4 * SROWS, WIDE), BF),
            pltpu.VMEM((4, NY, 2 * SROWS, WIDE), BF),
            pltpu.VMEM((1024, HALF), BF),
            pltpu.VMEM((HALF, 1024), BF),
            pltpu.VMEM((1024, QUARTER), BF),
            pltpu.VMEM((HALF, QUARTER), F32),
            pltpu.VMEM((2, 2, 4, 4 * BAND, HALF), BF),
            pltpu.VMEM((2, 2, 4, 4 * BAND, HALF), BF),
            pltpu.VMEM((4 * BAND, HALF), F32),
            pltpu.VMEM((4, 2, 2 * BAND, WIDE), BF),
            pltpu.VMEM((512, HALF), BF),
            pltpu.VMEM((NY, 768, 128), BF),
            dma((3,)), dma((11,)),
            dma((8,)), dma((8,)),
            dma((4, 4)), dma((4, 4)),
            dma((4,)), dma((4,)), dma((4,)), dma((4,)),
            dma((4, 4)), dma((4, 4)), dma((4, 4)), dma((4, 4)),
            dma((2, 2, 4)), dma((2, 2, 4)),
            dma((4, 2)), dma((4, 2)),
            dma((4,)), dma((4,)), dma((4, 4)), dma((4, 4)), dma((4, 4)), dma((4, 4)),
        ],
        compiler_params=pltpu.CompilerParams(
            collective_id=0, has_side_effects=True, vmem_limit_bytes=VMEM_A
        ),
        cost_estimate=pl.CostEstimate(flops=2 * 1024 * 768 * 1536, bytes_accessed=16 * 2**20, transcendentals=0),
    )(sm, sf, ss, ctx, og, nc)


def kernel_b(pc_in, lo_in, rx_in, gq_in, nm, nf, ns, wb_out, pc, lo, wb, rx, gq, vm, vf, vs, sem, out_sem, zbuf, obuf, gbuf, mbuf, fbuf, sbuf, starts):
    gq_copy = pltpu.make_async_copy(gq_in, gq, sem.at[0])
    rx_copies = [
        pltpu.make_async_copy(rx_in.at[pl.ds(i * 576, 576)], rx.at[pl.ds(i * 576, 576)], sem.at[1 + i])
        for i in range(4)
    ]
    small = [
        pltpu.make_async_copy(src, dst, sem.at[5 + i]) for i, (src, dst) in enumerate(((pc_in, pc), (lo_in, lo)))
    ]
    for copy in small:
        copy.start()
    gq_copy.start()
    for copy in rx_copies:
        copy.start()

    z = lax.rem(lax.axis_index("dp"), NZ)

    def count(j, total):
        starts[j] = total
        return total + pc[j]

    for copy in small:
        copy.wait()
    lax.fori_loop(0, 128, count, jnp.int32(0))

    gq_copy.wait()
    for yy in range(NY):
        for h in range(2):
            block = gq[yy, h].astype(F32)
            for q in range(2):
                c0 = yy * QUARTER + h * HALF + q * WIDE
                for n in range(3):
                    gbuf[c0 // 128 + n, 0:BAND, :] = block[q * BAND : (q + 1) * BAND, n * 128 : (n + 1) * 128]

    for i in range(4):
        rx_copies[i].wait()

        @pl.loop(i * 4, i * 4 + 4, unroll=2)
        def _(i):
            rows = pl.ds(i * 144, 144)
            value = rx[rows, :].astype(F32)
            for tile in range(3):
                zbuf[tile, rows, :] = value[:, tile * 128 : (tile + 1) * 128]

    lane = lax.broadcasted_iota(jnp.int32, (8, 128), 1)

    @pl.loop(0, 128, unroll=8)
    def _(i):
        rank = lo[i]
        start = starts[rank]
        length = pc[rank]
        tile = start // 128
        offset = lax.rem(start, 128)
        keep = (lane >= offset) & (lane < offset + length)
        spill = lane < offset + length - 128
        k = lax.rem(z + NZ - lax.rem(i // 4, NZ), NZ)
        far = k // 4
        pair = lax.rem(NY + (2 * far - 1) * k, NY)
        slot = (i // 32) * NZ + 2 * pair + far
        base = slot * SROWS + lax.rem(i, 4)
        for a in range(3):
            low, middle, high = (zbuf[tile, pl.ds(base + a * BAND, 8, stride=4), :] for tile in range(3))
            for r, value in enumerate(
                (low, jnp.where(lane >= 96, low, middle), jnp.where(lane >= 64, middle, high), high)
            ):
                value = pltpu.roll(value, lax.rem(offset + 32 * r, 128), 1)
                pltpu.store(obuf.at[a * 4 + r, tile], value, mask=keep)
                pltpu.store(obuf.at[a * 4 + r, tile + 1], value, mask=spill)

    def results(t):
        cols = pl.ds(pl.multiple_of(t * HALF, HALF), HALF)
        return [
            pltpu.make_async_copy(src.at[:, cols], dst.at[:, cols], out_sem.at[a, t])
            for a, (src, dst) in enumerate(((vm, nm), (vf, nf), (vs, ns)))
        ]

    @pl.loop(0, NT)
    def _(t):
        for c in range(6):
            n = t * 6 + c
            cols = pl.ds(pl.multiple_of(n * 128, 128), 128)
            for r in range(4):
                rows = pl.ds(r, 8, stride=4)
                gradient = gbuf[n, rows, :]
                first = 0.9 * obuf[4 + r, n] + 0.1 * gradient
                second = 0.95 * obuf[8 + r, n] + 0.05 * gradient * gradient
                master = obuf[r, n] - 0.01 * (first / first_bias) / (jnp.sqrt(second / second_bias) + 1e-08)
                mbuf[n, rows, :] = master
                fbuf[n, rows, :] = first
                sbuf[n, rows, :] = second
            vm[:, cols] = mbuf[n, 0:BAND, :]
            vf[:, cols] = fbuf[n, 0:BAND, :]
            vs[:, cols] = sbuf[n, 0:BAND, :]
        for copy in results(t):
            copy.start()
        for part in range(PARTS):
            wb[part, t] = jnp.concatenate(
                [mbuf[t * 6 + 2 * part, 0:BAND, :], mbuf[t * 6 + 2 * part + 1, 0:BAND, :]], axis=0
            ).astype(BF)

    weights = pltpu.make_async_copy(wb, wb_out.at[pl.ds(0, PARTS)], sem.at[7])
    weights.start()
    for t in range(NT):
        for copy in results(t):
            copy.wait()
    weights.wait()


def run_b(pc, lo, rx, gq):
    hbm = pl.BlockSpec(memory_space=pltpu.HBM)
    state = jax.ShapeDtypeStruct((BAND, 6144), F32)
    return pl.pallas_call(
        kernel_b,
        name="place_and_adam",
        out_shape=(state, state, state, jax.ShapeDtypeStruct((ROOM, NT, 2 * BAND, 128), BF)),
        in_specs=[hbm, hbm, hbm, hbm],
        out_specs=(hbm, hbm, hbm, hbm),
        scratch_shapes=[
            pltpu.SMEM((128,), jnp.int32),
            pltpu.SMEM((128,), jnp.int32),
            pltpu.VMEM((PARTS, NT, 2 * BAND, 128), BF),
            pltpu.VMEM((32 * SROWS, WIDE), BF),
            pltpu.VMEM((NY, 2, 2 * BAND, WIDE), BF),
            pltpu.VMEM((BAND, 6144), F32),
            pltpu.VMEM((BAND, 6144), F32),
            pltpu.VMEM((BAND, 6144), F32),
            pltpu.SemaphoreType.DMA((8,)),
            pltpu.SemaphoreType.DMA((3, NT)),
            pltpu.VMEM((3, 32 * SROWS + 32, 128), F32),
            pltpu.VMEM((12, 50, 8, 128), F32),
            pltpu.VMEM((48, 32, 128), F32),
            pltpu.VMEM((48, 32, 128), F32),
            pltpu.VMEM((48, 32, 128), F32),
            pltpu.VMEM((48, 32, 128), F32),
            pltpu.SMEM((128,), jnp.int32),
        ],
        compiler_params=pltpu.CompilerParams(vmem_limit_bytes=VMEM_B),
        cost_estimate=pl.CostEstimate(flops=10**9, bytes_accessed=5 * 2**20, transcendentals=0),
    )(pc, lo, rx, gq)


def kernel_c(
    wb, nc, out, wg, wa, wl, wh, nv, own, held, po, ro,
    nc_sem, own_sem, w1_s, w1_r, zz_s, zz_r, yo_s, yo_r,
):
    dp, t, y, z = where_am_i()
    load = pltpu.make_async_copy(nc, nv, nc_sem.at[0])
    load.start()
    own_in = pltpu.make_async_copy(wb.at[pl.ds(0, PARTS), t], wg.at[:, z, t], own_sem.at[0])
    own_in.start()

    barrier = pltpu.get_barrier_semaphore()
    for k in range(1, NT):
        pl.semaphore_signal(barrier, inc=1, device_id=(dp, lax.rem(t + k, NT)), device_id_type=MESH)
    for k in range(1, NY):
        pl.semaphore_signal(
            barrier, inc=1, device_id=(lax.rem(y + k, NY) * NZ + z, t), device_id_type=MESH
        )
    for k in (1, NZ - 1):
        pl.semaphore_signal(
            barrier, inc=1, device_id=(y * NZ + lax.rem(z + k, NZ), t), device_id_type=MESH
        )
    pl.semaphore_wait(barrier, NT - 1 + NY - 1 + 2)

    def first_copy(k, n):
        to = lax.rem(t + k, NT)
        return remote(wb.at[n, to], wg.at[n, z, t], w1_s.at[k, n], w1_r.at[k, n], (dp, to))

    for n in range(PARTS):
        for k in range(1, NT):
            first_copy(k, n).start()
    wl[...] = jnp.zeros_like(wl)
    wh[...] = jnp.zeros_like(wh)
    own_in.wait()

    def steps(d, part):
        return 4 if d == part % 2 else 3

    def around(d, s, n, part):
        sign = 1 if d == 0 else NZ - 1
        owner = lax.rem(z + (NZ - sign) * s, NZ)
        width = NT // SUBS[n]
        piece = wg.at[n, owner, pl.ds(part * width, width)]
        return remote(
            piece, piece, zz_s.at[d, s, n, part], zz_r.at[d, s, n, part],
            (y * NZ + lax.rem(z + sign, NZ), t),
        )

    def back(kind, n):
        to = lax.rem(y + (1 if kind % 2 == 0 else NY - 1), NY) * NZ + z
        return remote(po.at[n, kind], ro.at[n, kind], yo_s.at[kind, n], yo_r.at[kind, n], (to, t))

    def arrange(n):
        @pl.loop(0, NT)
        def _(tt):
            base = pl.multiple_of(tt * 128, 128)
            for pair in range(4):
                a = wg[n, 2 * pair, tt].astype(F32)
                b = wg[n, 2 * pair + 1, tt].astype(F32)
                for q in range(2):
                    rows = slice(q * BAND, (q + 1) * BAND)
                    cols = slice(q * 128, (q + 1) * 128)
                    both = jnp.concatenate([a[rows], b[rows]], axis=0).astype(BF)
                    if pair < 2:
                        wa[n, pl.ds(base + pair * 48, 48), cols] = both
                    elif pair == 2:
                        wa[n, pl.ds(base + 96, 32), cols] = both[:32]
                        wl[n, pl.ds(base, 16), cols] = both[32:]
                        wh[n, pl.ds(base + 64, 16), cols] = both[32:]
                    else:
                        wl[n, pl.ds(base + 16, 48), cols] = both
                        wh[n, pl.ds(base + 80, 48), cols] = both

    def product(n, k, half):
        ys = lax.rem(y + k, NY)
        value = jnp.dot(nv[ys, half * 256 : half * 256 + 256, :], wa[n], preferred_element_type=F32)
        tail = (wl, wh)[half]
        return value + jnp.dot(nv[ys, 512:768, :], tail[n], preferred_element_type=F32)

    def multiply(n):
        for kind, k, half in ((0, 2, 0), (1, 2, 1), (2, 1, 1), (3, 3, 0)):
            po[n, kind] = product(n, k, half).astype(BF)
            back(kind, n).start()
        held[n, 0] = product(n, 1, 0)
        held[n, 1] = product(n, 3, 1)
        own[n, 0:256, :] = product(n, 0, 0)
        own[n, 256:512, :] = product(n, 0, 1)

    def join(n):
        for d in range(2):
            back(d, n).wait_recv()
            po[n, 4 + d] = (held[n, d] + ro[n, d].astype(F32)).astype(BF)
            back(4 + d, n).start()

    for tick in range(6 + STAGGER * (PARTS - 1)):
        for n in range(PARTS):
            s = tick - STAGGER * n
            if s == 0:
                for k in range(1, NT):
                    first_copy(k, n).wait_recv()
            for part in range(SUBS[n]):
                for d in range(2):
                    if s > 0 and s - 1 < steps(d, part):
                        around(d, s - 1, n, part).wait_recv()
                    if 0 <= s < steps(d, part):
                        around(d, s, n, part).start()
        for n in range(PARTS):
            if tick - STAGGER * n == 4:
                if n == 0:
                    load.wait()
                arrange(n)
                multiply(n)
            if tick - STAGGER * n == 5:
                join(n)

    for n in range(PARTS):
        cols = slice(n * 256, (n + 1) * 256)
        for half, kinds in ((0, (3, 4)), (1, (2, 5))):
            rows = slice(half * 256, half * 256 + 256)
            value = own[n, rows, :]
            for kind in kinds:
                back(kind, n).wait_recv()
                value = value + ro[n, kind].astype(F32)
            out[rows, cols] = value.astype(BF)

    for n in range(PARTS):
        for k in range(1, NT):
            first_copy(k, n).wait_send()
        for d in range(2):
            for part in range(SUBS[n]):
                for s in range(steps(d, part)):
                    around(d, s, n, part).wait_send()
        for kind in range(6):
            back(kind, n).wait_send()


def run_c(wb, nc):
    hbm = pl.BlockSpec(memory_space=pltpu.HBM)
    vmem = pl.BlockSpec(memory_space=pltpu.VMEM)
    dma = pltpu.SemaphoreType.DMA
    return pl.pallas_call(
        kernel_c,
        name="weights_and_product",
        out_shape=jax.ShapeDtypeStruct((512, HALF), BF),
        in_specs=[hbm, hbm],
        out_specs=vmem,
        scratch_shapes=[
            pltpu.VMEM((PARTS, NZ, NT, 2 * BAND, 128), BF),
            pltpu.VMEM((PARTS, 1024, 256), BF),
            pltpu.VMEM((PARTS, 1024, 256), BF),
            pltpu.VMEM((PARTS, 1024, 256), BF),
            pltpu.VMEM((NY, 768, 1024), BF),
            pltpu.VMEM((PARTS, 512, 256), F32),
            pltpu.VMEM((PARTS, 2, 256, 256), F32),
            pltpu.VMEM((PARTS, 6, 256, 256), BF),
            pltpu.VMEM((PARTS, 6, 256, 256), BF),
            dma((1,)), dma((1,)),
            dma((8, PARTS)), dma((8, PARTS)),
            dma((2, 4, PARTS, 4)), dma((2, 4, PARTS, 4)),
            dma((6, PARTS)), dma((6, PARTS)),
        ],
        compiler_params=pltpu.CompilerParams(
            collective_id=1, has_side_effects=True, vmem_limit_bytes=VMEM_C
        ),
        cost_estimate=pl.CostEstimate(flops=2 * 512 * 6144 * 768, bytes_accessed=8 * 2**20, transcendentals=0),
    )(wb, nc)


def shards(
    saved_master,
    saved_first,
    saved_second,
    piece_columns,
    load_order,
    context,
    out_grad,
    next_context,
):
    def grouped(saved):
        return saved[0].reshape(4, 192, WIDE).transpose(1, 0, 2)

    rx, gq, tokens = run_a(
        grouped(saved_master), grouped(saved_first), grouped(saved_second), context, out_grad, next_context
    )
    new_master, new_first, new_second, blocks = run_b(
        piece_columns[0], load_order[0], rx.reshape(32 * SROWS, WIDE), gq
    )
    activations = run_c(blocks, tokens)
    return (new_master, new_first, new_second, activations)


def solution(mesh):
    placed = (
        P("tensor", "dp", None),
        P("tensor", "dp", None),
        P("tensor", "dp", None),
        P("tensor", None),
        P("tensor", None),
        P("dp", "tensor"),
        P("dp", None),
        P("dp", "tensor"),
    )
    return jax.shard_map(
        shards,
        mesh=mesh,
        in_specs=placed,
        out_specs=(
            P(("tensor", "dp"), None),
            P(("tensor", "dp"), None),
            P(("tensor", "dp"), None),
            P("dp", "tensor"),
        ),
        check_vma=False,
    )
```

```python
import jax
import jax.numpy as jnp
from jax import lax
from jax.experimental import pallas as pl
from jax.experimental.pallas import tpu as pltpu
from jax.sharding import PartitionSpec as P

first_bias = 1.0 - 0.9**20
second_bias = 1.0 - 0.95**20

MESH = pl.DeviceIdType.MESH
BF = jnp.bfloat16
F32 = jnp.float32
NY, NZ = 4, 8
NT = 8
BAND = 24
WIDE = 384
GROUPS = 6
SROWS = 72
QUARTER = 1536
HALF = 768


def where_am_i():
    dp = lax.axis_index("dp")
    t = lax.axis_index("tensor")
    return dp, t, dp // NZ, lax.rem(dp, NZ)


def remote(src, dst, send, recv, device):
    return pltpu.make_async_remote_copy(
        src_ref=src, dst_ref=dst, send_sem=send, recv_sem=recv, device_id=device, device_id_type=MESH
    )


SUBS = (4, 4, 4)
STARTS = (0, 2, 4)
ROOM = 32
PARTS = 3
VMEM_A = 60 * 2**20
VMEM_C = 104 * 2**19
VMEM_B = 60 * 2**20


def kernel_a(
    sm, sf, ss, ctx, og, nc, rx, gq, nv,
    st, flat, tx, mid, ty, cg, ct, oq, grad, zs, zr, tot, ysb, nraw, nsend,
    load_sem, loc_sem, st_s, st_r, sy_s, sy_r, cx_s, cx_r, og_s, og_r, ox_s, ox_r, om_s, om_r, rs_s, rs_r, ya_s, ya_r,
    ny_s, ny_r, nx_s, nx_r, nm_s, nm_r,
):
    dp, t, y, z = where_am_i()
    core = lax.rem(t, 2)
    mate = t + 1 - 2 * core

    loads = [pltpu.make_async_copy(src, st.at[a], load_sem.at[a]) for a, src in enumerate((sm, sf, ss))]
    for copy in loads:
        copy.start()
    own_ctx = pltpu.make_async_copy(ctx, cg.at[pl.ds(y * 256, 256)], loc_sem.at[0])
    own_og = pltpu.make_async_copy(
        og.at[:, pl.ds(y * QUARTER, QUARTER)], oq.at[pl.ds(y * 256, 256)], loc_sem.at[1]
    )
    tokens_in = pltpu.make_async_copy(nc, nraw, loc_sem.at[9])
    tokens_in.start()
    own_ctx.start()
    own_og.start()

    barrier = pltpu.get_barrier_semaphore()

    for k in range(1, NY):
        pl.semaphore_signal(
            barrier, inc=1, device_id=(lax.rem(y + k, NY) * NZ + z, t), device_id_type=MESH
        )
    for k in range(1, NZ):
        pl.semaphore_signal(
            barrier, inc=1, device_id=(y * NZ + lax.rem(z + k, NZ), t), device_id_type=MESH
        )
    for k in range(1, 4):
        pl.semaphore_signal(barrier, inc=1, device_id=(dp, lax.rem(t + 2 * k, NT)), device_id_type=MESH)
    pl.semaphore_signal(barrier, inc=1, device_id=(dp, mate), device_id_type=MESH)
    pl.semaphore_wait(barrier, NY - 1 + NZ - 1 + 3 + 1)

    def ctx_copy(k):
        to = lax.rem(y + k, NY)
        return remote(ctx, cg.at[pl.ds(y * 256, 256)], cx_s.at[k], cx_r.at[k], (to * NZ + z, t))

    def og_copy(k):
        to = lax.rem(y + k, NY)
        return remote(
            og.at[pl.ds(t * 32, 32), pl.ds(to * QUARTER, QUARTER)],
            oq.at[pl.ds(y * 256 + t * 32, 32)],
            og_s.at[k], og_r.at[k], (to * NZ + z, t),
        )

    def og_rows(k, tt):
        return oq.at[pl.ds(lax.rem(y + NY - k, NY) * 256 + tt * 32, 32)]

    def og_over_x(k, kx):
        piece = og_rows(k, t)
        return remote(piece, piece, ox_s.at[k, kx], ox_r.at[k, kx], (dp, lax.rem(t + 2 * kx, NT)))

    def og_to_mate(k, kx):
        piece = og_rows(k, lax.rem(t + NT - 2 * kx, NT))
        return remote(piece, piece, om_s.at[k, kx], om_r.at[k, kx], (dp, mate))

    def lanes(tt):
        return pl.ds(pl.multiple_of(tt * 128, 128), 128)

    def tokens_over_y(k):
        to = lax.rem(y + k, NY)
        return remote(
            nsend.at[to], nv.at[y, :, lanes(t)], ny_s.at[k], ny_r.at[k], (to * NZ + z, t)
        )

    def tokens_over_x(k, kx):
        piece = nv.at[lax.rem(y + NY - k, NY), :, lanes(t)]
        return remote(
            piece if k else nsend.at[y], piece, nx_s.at[k, kx], nx_r.at[k, kx], (dp, lax.rem(t + 2 * kx, NT))
        )

    def tokens_to_mate(k, kx):
        piece = nv.at[lax.rem(y + NY - k, NY), :, lanes(lax.rem(t + NT - 2 * kx, NT))]
        return remote(
            piece if k or kx else nsend.at[y], piece, nm_s.at[k, kx], nm_r.at[k, kx], (dp, mate)
        )

    def tokens_onward(k):
        for kx in (2, 1, 3):
            tokens_over_x(k, kx).start()
        tokens_to_mate(k, 0).start()

    def tokens_passed(k):
        for kx in (1, 3, 2):
            tokens_over_x(k, kx).wait_recv()
            tokens_to_mate(k, kx).start()

    for k in (2, 1, 3):
        og_copy(k).start()
    own_tokens = pltpu.make_async_copy(nsend.at[y], nv.at[y, :, lanes(t)], loc_sem.at[10])
    tokens_in.wait()
    for yy in range(NY):
        c0 = yy * 192
        nsend[yy, 0:512, :] = nraw[:, c0 : c0 + 128]
        tail = nraw[:, c0 + 128 : c0 + 192]
        nsend[yy, 512:768, :] = jnp.concatenate([tail[:256], tail[256:]], axis=1)
    for k in (2, 1, 3):
        tokens_over_y(k).start()
    own_tokens.start()
    tokens_onward(0)
    for k in (2, 1, 3):
        ctx_copy(k).start()

    for copy in loads:
        copy.wait()

    def state_copy(k):
        to = lax.rem(z + k, NZ)
        return remote(tx.at[k], mid.at[k], st_s.at[k], st_r.at[k], (y * NZ + to, t))

    def build(k):
        for ky in range(NY):
            owner = lax.rem(y + ky, NY) * NZ + lax.rem(z + k, NZ)
            for a in range(3):
                for g in range(GROUPS):
                    row = ky * SROWS + a * BAND + 4 * g
                    flat[row : row + 4, :] = st[a, owner * GROUPS + g]
        return flat[...].astype(BF)

    for k in (4, 3, 5, 2, 6, 1, 7):
        tx[k] = build(k)
        state_copy(k).start()
    mid[0] = build(0)

    def state_over_y(k, pair):
        to = lax.rem(y + k, NY) * NZ + z
        return remote(ty.at[pair, k], rx.at[y * 4 + pair], sy_s.at[pair, k], sy_r.at[pair, k], (to, t))

    def state_local(pair):
        return pltpu.make_async_copy(ty.at[pair, 0], rx.at[y * 4 + pair], loc_sem.at[5 + pair])

    def pass_state(pair):
        first, second = ((0, 4), (3, 5), (2, 6), (1, 7))[pair]
        if first:
            state_copy(first).wait_recv()
        state_copy(second).wait_recv()
        low = mid[first].astype(F32)
        high = mid[second].astype(F32)
        for k in (2, 1, 3, 0):
            rows = slice(k * SROWS, (k + 1) * SROWS)
            ty[pair, k] = jnp.concatenate([low[rows], high[rows]], axis=0).astype(BF)
            if k:
                state_over_y(k, pair).start()
            else:
                state_local(pair).start()

    for k in (1, 3, 2):
        og_copy(k).wait_recv()
        for kx in (2, 1, 3):
            og_over_x(k, kx).start()
        og_to_mate(k, 0).start()
    for k in (1, 3, 2):
        tokens_over_y(k).wait_recv()
        tokens_onward(k)

    own_ctx.wait()
    own_og.wait()

    def turn(source):
        ct[:, pl.ds(source * 256, 256)] = cg[pl.ds(source * 256, 256), :].T

    turn(y)
    for k in (1, 3, 2):
        ctx_copy(k).wait_recv()
        turn(lax.rem(y + NY - k, NY))
    for k in (1, 3, 2):
        for kx in (1, 3, 2):
            og_over_x(k, kx).wait_recv()
            og_to_mate(k, kx).start()
    for k in (1, 3, 2):
        for kx in range(4):
            og_to_mate(k, kx).wait_recv()

    def chunk(dest, h):
        return jnp.concatenate(
            [grad[pl.ds((yy * NZ + dest) * BAND, BAND), h * HALF : (h + 1) * HALF] for yy in range(NY)], axis=0
        )

    def steps(d, h):
        return 4 if d == h else 3

    def ring_copy(d, h, s):
        to = lax.rem(z + (1 if d == 0 else NZ - 1), NZ)
        return remote(zs.at[d, h, s], zr.at[d, h, s], rs_s.at[d, h, s], rs_r.at[d, h, s], (y * NZ + to, t))

    def ring_send(d, h, s):
        sign = 1 if d == 0 else NZ - 1
        dest = lax.rem(z + sign * (steps(d, h) - s), NZ)
        value = chunk(dest, h)
        if s > 0:
            ring_copy(d, h, s - 1).wait_recv()
            value = value + zr[d, h, s - 1].astype(F32)
        zs[d, h, s] = value.astype(BF)
        ring_copy(d, h, s).start()

    for h in range(2):
        @pl.loop(0, 3)
        def _(n):
            cols = pl.ds(h * HALF + n * 256, 256)
            grad[:, cols] = jnp.dot(ct[...], oq[:, cols], preferred_element_type=F32)

        ring_send(h, h, 0)
        ring_send(1 - h, h, 0)

    pass_state(0)
    tokens_passed(0)
    for s in range(1, 4):
        for h in range(2):
            for d in (h, 1 - h):
                if s < steps(d, h):
                    ring_send(d, h, s)
        for pair in ((1, 2), (3,), ())[s - 1]:
            pass_state(pair)
        for k in ((), (1,), (3,))[s - 1]:
            tokens_passed(k)

    def out_copy(k, h):
        to = lax.rem(y + k, NY)
        return remote(ysb.at[k, h], gq.at[y, h], ya_s.at[k, h], ya_r.at[k, h], (to * NZ + z, t))

    own_out = []
    for h in range(2):
        value = chunk(z, h)
        for d in (1 - h, h):
            last = steps(d, h) - 1
            ring_copy(d, h, last).wait_recv()
            value = value + zr[d, h, last].astype(F32)
        tot[...] = value
        for k in (2, 1, 3, 0):
            rows = pl.ds(lax.rem(y + k, NY) * BAND, BAND)
            ysb[k, h] = jnp.concatenate([tot[rows, 0:WIDE], tot[rows, WIDE:HALF]], axis=0).astype(BF)
            if k:
                out_copy(k, h).start()
            else:
                own_out.append(pltpu.make_async_copy(ysb.at[0, h], gq.at[y, h], loc_sem.at[3 + h]))
                own_out[-1].start()

    tokens_passed(2)
    for k in (1, 2, 3):
        og_copy(k).wait_send()
        ctx_copy(k).wait_send()
        for kx in (1, 2, 3):
            og_over_x(k, kx).wait_send()
        for kx in range(4):
            og_to_mate(k, kx).wait_send()
    for h in range(2):
        for d in range(2):
            for s in range(steps(d, h)):
                ring_copy(d, h, s).wait_send()
        for k in (1, 2, 3):
            out_copy(k, h).wait()
        own_out[h].wait()
    for k in range(1, NZ):
        state_copy(k).wait_send()
    for k in range(1, 4):
        tokens_over_y(k).wait_send()
    own_tokens.wait()
    for k in range(4):
        for kx in range(1, 4):
            tokens_over_x(k, kx).wait_send()
        for kx in range(4):
            tokens_to_mate(k, kx).wait()
    for pair in range(4):
        for k in (1, 2, 3):
            state_over_y(k, pair).wait()
        state_local(pair).wait()


def run_a(sm, sf, ss, ctx, og, nc):
    hbm = pl.BlockSpec(memory_space=pltpu.HBM)
    dma = pltpu.SemaphoreType.DMA
    return pl.pallas_call(
        kernel_a,
        name="state_and_gradient",
        out_shape=(
            jax.ShapeDtypeStruct((16, 2 * SROWS, WIDE), BF),
            jax.ShapeDtypeStruct((NY, 2, 2 * BAND, WIDE), BF),
            jax.ShapeDtypeStruct((NY, 768, 1024), BF),
        ),
        in_specs=[hbm] * 6,
        out_specs=(hbm, hbm, hbm),
        scratch_shapes=[
            pltpu.VMEM((3, 192, 4, WIDE), F32),
            pltpu.VMEM((4 * SROWS, WIDE), F32),
            pltpu.VMEM((NZ, 4 * SROWS, WIDE), BF),
            pltpu.VMEM((NZ, 4 * SROWS, WIDE), BF),
            pltpu.VMEM((4, NY, 2 * SROWS, WIDE), BF),
            pltpu.VMEM((1024, HALF), BF),
            pltpu.VMEM((HALF, 1024), BF),
            pltpu.VMEM((1024, QUARTER), BF),
            pltpu.VMEM((HALF, QUARTER), F32),
            pltpu.VMEM((2, 2, 4, 4 * BAND, HALF), BF),
            pltpu.VMEM((2, 2, 4, 4 * BAND, HALF), BF),
            pltpu.VMEM((4 * BAND, HALF), F32),
            pltpu.VMEM((4, 2, 2 * BAND, WIDE), BF),
            pltpu.VMEM((512, HALF), BF),
            pltpu.VMEM((NY, 768, 128), BF),
            dma((3,)), dma((11,)),
            dma((8,)), dma((8,)),
            dma((4, 4)), dma((4, 4)),
            dma((4,)), dma((4,)), dma((4,)), dma((4,)),
            dma((4, 4)), dma((4, 4)), dma((4, 4)), dma((4, 4)),
            dma((2, 2, 4)), dma((2, 2, 4)),
            dma((4, 2)), dma((4, 2)),
            dma((4,)), dma((4,)), dma((4, 4)), dma((4, 4)), dma((4, 4)), dma((4, 4)),
        ],
        compiler_params=pltpu.CompilerParams(
            collective_id=0, has_side_effects=True, vmem_limit_bytes=VMEM_A
        ),
        cost_estimate=pl.CostEstimate(flops=2 * 1024 * 768 * 1536, bytes_accessed=16 * 2**20, transcendentals=0),
    )(sm, sf, ss, ctx, og, nc)


def kernel_b(pc_in, lo_in, rx_in, gq_in, nm, nf, ns, wb_out, pc, lo, wb, rx, gq, vm, vf, vs, sem, out_sem, zbuf, obuf, gbuf, mbuf, fbuf, sbuf, starts):
    gq_copy = pltpu.make_async_copy(gq_in, gq, sem.at[0])
    rx_copies = [
        pltpu.make_async_copy(rx_in.at[pl.ds(i * 576, 576)], rx.at[pl.ds(i * 576, 576)], sem.at[1 + i])
        for i in range(4)
    ]
    small = [
        pltpu.make_async_copy(src, dst, sem.at[5 + i]) for i, (src, dst) in enumerate(((pc_in, pc), (lo_in, lo)))
    ]
    for copy in small:
        copy.start()
    gq_copy.start()
    for copy in rx_copies:
        copy.start()

    z = lax.rem(lax.axis_index("dp"), NZ)

    def count(j, total):
        starts[j] = total
        return total + pc[j]

    for copy in small:
        copy.wait()
    lax.fori_loop(0, 128, count, jnp.int32(0))

    gq_copy.wait()
    for yy in range(NY):
        for h in range(2):
            block = gq[yy, h].astype(F32)
            for q in range(2):
                c0 = yy * QUARTER + h * HALF + q * WIDE
                for n in range(3):
                    gbuf[c0 // 128 + n, 0:BAND, :] = block[q * BAND : (q + 1) * BAND, n * 128 : (n + 1) * 128]

    for i in range(4):
        rx_copies[i].wait()

        @pl.loop(i * 4, i * 4 + 4, unroll=2)
        def _(i):
            rows = pl.ds(i * 144, 144)
            value = rx[rows, :].astype(F32)
            for tile in range(3):
                zbuf[tile, rows, :] = value[:, tile * 128 : (tile + 1) * 128]

    lane = lax.broadcasted_iota(jnp.int32, (8, 128), 1)

    @pl.loop(0, 128, unroll=8)
    def _(i):
        rank = lo[i]
        start = starts[rank]
        length = pc[rank]
        tile = start >> 7
        offset = start & 127
        keep = (lane >= offset) & (lane < offset + length)
        spill = lane < offset + length - 128
        k = (z - (i >> 2)) & 7
        far = k >> 2
        pair = ((2 * far - 1) * k) & 3
        slot = (i >> 5) * NZ + 2 * pair + far
        base = slot * SROWS + (i & 3)
        for a in range(3):
            low, middle, high = (zbuf[tile, pl.ds(base + a * BAND, 8, stride=4), :] for tile in range(3))
            for r, value in enumerate(
                (low, jnp.where(lane >= 96, low, middle), jnp.where(lane >= 64, middle, high), high)
            ):
                value = pltpu.roll(value, (offset + 32 * r) & 127, 1)
                pltpu.store(obuf.at[a * 4 + r, tile], value, mask=keep)
                pltpu.store(obuf.at[a * 4 + r, tile + 1], value, mask=spill)

    def results(t):
        cols = pl.ds(pl.multiple_of(t * HALF, HALF), HALF)
        return [
            pltpu.make_async_copy(src.at[:, cols], dst.at[:, cols], out_sem.at[a, t])
            for a, (src, dst) in enumerate(((vm, nm), (vf, nf), (vs, ns)))
        ]

    @pl.loop(0, NT)
    def _(t):
        for c in range(6):
            n = t * 6 + c
            cols = pl.ds(pl.multiple_of(n * 128, 128), 128)
            for r in range(4):
                rows = pl.ds(r, 8, stride=4)
                gradient = gbuf[n, rows, :]
                first = 0.9 * obuf[4 + r, n] + 0.1 * gradient
                second = 0.95 * obuf[8 + r, n] + 0.05 * gradient * gradient
                master = obuf[r, n] - 0.01 * (first / first_bias) / (jnp.sqrt(second / second_bias) + 1e-08)
                mbuf[n, rows, :] = master
                fbuf[n, rows, :] = first
                sbuf[n, rows, :] = second
            vm[:, cols] = mbuf[n, 0:BAND, :]
            vf[:, cols] = fbuf[n, 0:BAND, :]
            vs[:, cols] = sbuf[n, 0:BAND, :]
        for copy in results(t):
            copy.start()
        for part in range(PARTS):
            wb[part, t] = jnp.concatenate(
                [mbuf[t * 6 + 2 * part, 0:BAND, :], mbuf[t * 6 + 2 * part + 1, 0:BAND, :]], axis=0
            ).astype(BF)

    weights = pltpu.make_async_copy(wb, wb_out.at[pl.ds(0, PARTS)], sem.at[7])
    weights.start()
    for t in range(NT):
        for copy in results(t):
            copy.wait()
    weights.wait()


def run_b(pc, lo, rx, gq):
    hbm = pl.BlockSpec(memory_space=pltpu.HBM)
    state = jax.ShapeDtypeStruct((BAND, 6144), F32)
    return pl.pallas_call(
        kernel_b,
        name="place_and_adam",
        out_shape=(state, state, state, jax.ShapeDtypeStruct((ROOM, NT, 2 * BAND, 128), BF)),
        in_specs=[hbm, hbm, hbm, hbm],
        out_specs=(hbm, hbm, hbm, hbm),
        scratch_shapes=[
            pltpu.SMEM((128,), jnp.int32),
            pltpu.SMEM((128,), jnp.int32),
            pltpu.VMEM((PARTS, NT, 2 * BAND, 128), BF),
            pltpu.VMEM((32 * SROWS, WIDE), BF),
            pltpu.VMEM((NY, 2, 2 * BAND, WIDE), BF),
            pltpu.VMEM((BAND, 6144), F32),
            pltpu.VMEM((BAND, 6144), F32),
            pltpu.VMEM((BAND, 6144), F32),
            pltpu.SemaphoreType.DMA((8,)),
            pltpu.SemaphoreType.DMA((3, NT)),
            pltpu.VMEM((3, 32 * SROWS + 32, 128), F32),
            pltpu.VMEM((12, 50, 8, 128), F32),
            pltpu.VMEM((48, 32, 128), F32),
            pltpu.VMEM((48, 32, 128), F32),
            pltpu.VMEM((48, 32, 128), F32),
            pltpu.VMEM((48, 32, 128), F32),
            pltpu.SMEM((128,), jnp.int32),
        ],
        compiler_params=pltpu.CompilerParams(vmem_limit_bytes=VMEM_B),
        cost_estimate=pl.CostEstimate(flops=10**9, bytes_accessed=5 * 2**20, transcendentals=0),
    )(pc, lo, rx, gq)


def kernel_c(
    wb, nc, out, wg, wa, wl, wh, nv, own, held, po, ro,
    nc_sem, own_sem, w1_s, w1_r, zz_s, zz_r, yo_s, yo_r,
):
    dp, t, y, z = where_am_i()
    load = pltpu.make_async_copy(nc, nv, nc_sem.at[0])
    load.start()
    own_in = pltpu.make_async_copy(wb.at[pl.ds(0, PARTS), t], wg.at[:, z, t], own_sem.at[0])
    own_in.start()

    barrier = pltpu.get_barrier_semaphore()
    for k in range(1, NT):
        pl.semaphore_signal(barrier, inc=1, device_id=(dp, lax.rem(t + k, NT)), device_id_type=MESH)
    for k in range(1, NY):
        pl.semaphore_signal(
            barrier, inc=1, device_id=(lax.rem(y + k, NY) * NZ + z, t), device_id_type=MESH
        )
    for k in (1, NZ - 1):
        pl.semaphore_signal(
            barrier, inc=1, device_id=(y * NZ + lax.rem(z + k, NZ), t), device_id_type=MESH
        )
    pl.semaphore_wait(barrier, NT - 1 + NY - 1 + 2)

    def first_copy(k, n):
        to = lax.rem(t + k, NT)
        return remote(wb.at[n, to], wg.at[n, z, t], w1_s.at[k, n], w1_r.at[k, n], (dp, to))

    for n in range(PARTS):
        for k in range(1, NT):
            first_copy(k, n).start()
    wl[...] = jnp.zeros_like(wl)
    wh[...] = jnp.zeros_like(wh)
    own_in.wait()

    def steps(d, part):
        return 4 if d == part % 2 else 3

    def around(d, s, n, part):
        sign = 1 if d == 0 else NZ - 1
        owner = lax.rem(z + (NZ - sign) * s, NZ)
        width = NT // SUBS[n]
        piece = wg.at[n, owner, pl.ds(part * width, width)]
        return remote(
            piece, piece, zz_s.at[d, s, n, part], zz_r.at[d, s, n, part],
            (y * NZ + lax.rem(z + sign, NZ), t),
        )

    def back(kind, n):
        to = lax.rem(y + (1 if kind % 2 == 0 else NY - 1), NY) * NZ + z
        return remote(po.at[n, kind], ro.at[n, kind], yo_s.at[kind, n], yo_r.at[kind, n], (to, t))

    def arrange(n):
        @pl.loop(0, NT)
        def _(tt):
            base = pl.multiple_of(tt * 128, 128)
            for pair in range(4):
                a = wg[n, 2 * pair, tt].astype(F32)
                b = wg[n, 2 * pair + 1, tt].astype(F32)
                for q in range(2):
                    rows = slice(q * BAND, (q + 1) * BAND)
                    cols = slice(q * 128, (q + 1) * 128)
                    both = jnp.concatenate([a[rows], b[rows]], axis=0).astype(BF)
                    if pair < 2:
                        wa[n, pl.ds(base + pair * 48, 48), cols] = both
                    elif pair == 2:
                        wa[n, pl.ds(base + 96, 32), cols] = both[:32]
                        wl[n, pl.ds(base, 16), cols] = both[32:]
                        wh[n, pl.ds(base + 64, 16), cols] = both[32:]
                    else:
                        wl[n, pl.ds(base + 16, 48), cols] = both
                        wh[n, pl.ds(base + 80, 48), cols] = both

    def product(n, k, half):
        ys = lax.rem(y + k, NY)
        value = jnp.dot(nv[ys, half * 256 : half * 256 + 256, :], wa[n], preferred_element_type=F32)
        tail = (wl, wh)[half]
        return value + jnp.dot(nv[ys, 512:768, :], tail[n], preferred_element_type=F32)

    def multiply(n):
        for kind, k, half in ((0, 2, 0), (1, 2, 1), (2, 1, 1), (3, 3, 0)):
            po[n, kind] = product(n, k, half).astype(BF)
            back(kind, n).start()
        held[n, 0] = product(n, 1, 0)
        held[n, 1] = product(n, 3, 1)
        own[n, 0:256, :] = product(n, 0, 0)
        own[n, 256:512, :] = product(n, 0, 1)

    def join(n):
        for d in range(2):
            back(d, n).wait_recv()
            po[n, 4 + d] = (held[n, d] + ro[n, d].astype(F32)).astype(BF)
            back(4 + d, n).start()

    for tick in range(6 + STARTS[-1]):
        for n in range(PARTS):
            s = tick - STARTS[n]
            if s == 0:
                for k in range(1, NT):
                    first_copy(k, n).wait_recv()
            for part in range(SUBS[n]):
                for d in range(2):
                    if s > 0 and s - 1 < steps(d, part):
                        around(d, s - 1, n, part).wait_recv()
                    if 0 <= s < steps(d, part):
                        around(d, s, n, part).start()
        for n in range(PARTS):
            if tick - STARTS[n] == 4:
                if n == 0:
                    load.wait()
                arrange(n)
                multiply(n)
            if tick - STARTS[n] == 5:
                join(n)

    for n in range(PARTS):
        cols = slice(n * 256, (n + 1) * 256)
        for half, kinds in ((0, (3, 4)), (1, (2, 5))):
            rows = slice(half * 256, half * 256 + 256)
            value = own[n, rows, :]
            for kind in kinds:
                back(kind, n).wait_recv()
                value = value + ro[n, kind].astype(F32)
            out[rows, cols] = value.astype(BF)

    for n in range(PARTS):
        for k in range(1, NT):
            first_copy(k, n).wait_send()
        for d in range(2):
            for part in range(SUBS[n]):
                for s in range(steps(d, part)):
                    around(d, s, n, part).wait_send()
        for kind in range(6):
            back(kind, n).wait_send()


def run_c(wb, nc):
    hbm = pl.BlockSpec(memory_space=pltpu.HBM)
    vmem = pl.BlockSpec(memory_space=pltpu.VMEM)
    dma = pltpu.SemaphoreType.DMA
    return pl.pallas_call(
        kernel_c,
        name="weights_and_product",
        out_shape=jax.ShapeDtypeStruct((512, HALF), BF),
        in_specs=[hbm, hbm],
        out_specs=vmem,
        scratch_shapes=[
            pltpu.VMEM((PARTS, NZ, NT, 2 * BAND, 128), BF),
            pltpu.VMEM((PARTS, 1024, 256), BF),
            pltpu.VMEM((PARTS, 1024, 256), BF),
            pltpu.VMEM((PARTS, 1024, 256), BF),
            pltpu.VMEM((NY, 768, 1024), BF),
            pltpu.VMEM((PARTS, 512, 256), F32),
            pltpu.VMEM((PARTS, 2, 256, 256), F32),
            pltpu.VMEM((PARTS, 6, 256, 256), BF),
            pltpu.VMEM((PARTS, 6, 256, 256), BF),
            dma((1,)), dma((1,)),
            dma((8, PARTS)), dma((8, PARTS)),
            dma((2, 4, PARTS, 4)), dma((2, 4, PARTS, 4)),
            dma((6, PARTS)), dma((6, PARTS)),
        ],
        compiler_params=pltpu.CompilerParams(
            collective_id=1, has_side_effects=True, vmem_limit_bytes=VMEM_C
        ),
        cost_estimate=pl.CostEstimate(flops=2 * 512 * 6144 * 768, bytes_accessed=8 * 2**20, transcendentals=0),
    )(wb, nc)


def shards(
    saved_master,
    saved_first,
    saved_second,
    piece_columns,
    load_order,
    context,
    out_grad,
    next_context,
):
    def grouped(saved):
        return saved[0].reshape(4, 192, WIDE).transpose(1, 0, 2)

    rx, gq, tokens = run_a(
        grouped(saved_master), grouped(saved_first), grouped(saved_second), context, out_grad, next_context
    )
    new_master, new_first, new_second, blocks = run_b(
        piece_columns[0], load_order[0], rx.reshape(32 * SROWS, WIDE), gq
    )
    activations = run_c(blocks, tokens)
    return (new_master, new_first, new_second, activations)


def solution(mesh):
    placed = (
        P("tensor", "dp", None),
        P("tensor", "dp", None),
        P("tensor", "dp", None),
        P("tensor", None),
        P("tensor", None),
        P("dp", "tensor"),
        P("dp", None),
        P("dp", "tensor"),
    )
    return jax.shard_map(
        shards,
        mesh=mesh,
        in_specs=placed,
        out_specs=(
            P(("tensor", "dp"), None),
            P(("tensor", "dp"), None),
            P(("tensor", "dp"), None),
            P("dp", "tensor"),
        ),
        check_vma=False,
    )
```
